32 devices in a mesh: groups: 2 (over y), fsdp: 8 (over z, x), tp: 2 (over core).
Axes of the slice: x: 2, y: 2, z: 4, core: 2. Of those that a mesh axis runs over, the one named last changes fastest.
Arguments:
- hidden: bfloat16 [4096, 8192], P(('groups', 'fsdp'), 'tp'), parts along dimension 0, may hold values from -6 to 6
- queries: bfloat16 [4096, 8192], P(('groups', 'fsdp'), 'tp'), parts along dimension 0, may hold values from -360 to 360
- lengths: int32 [16, 4], P(('groups', 'fsdp')), parts along dimension 0, may hold values from 1 to 128, 256 in all within a row
- scoring_rank: int32 [4096, 1], P(('groups', 'fsdp')), parts along dimension 0, may hold values from 0 to 7; in each aligned block of 256 rows (0 to 255, 256 to 511, ...) at most 64 rows name the same one
- norm_gain: float32 [8192], P('tp'), may hold values from 0.1 to 1.9
- kv_weight: bfloat16 [8192, 2048], P('fsdp', 'tp'), may hold values from -0.0625 to 0.0625
- kv_bias: float32 [2048], P('tp'), may hold values from -3 to 3
Outputs:
- attended: bfloat16 [4096, 8192], P(('groups', 'fsdp'), 'tp'), parts along dimension 0
- scored_rows: bfloat16 [8192, 2048], P(('groups', 'fsdp'), 'tp'), parts along dimension 0
The draws below stay inside these ranges and needn't reach their ends.
There are 2 independent parts, one for each index of `groups`. The reference program is written for one: setup_inputs(seed, part) draws one part's arguments, and reference() takes and returns one part's arrays. A program takes and returns all parts, laid end to end along the dimension named above; an argument that names none is the same for every part. Nothing has to cross between parts.
Inputs may be any that keep to these rules, and one draw needn't show every extreme that they name: `scoring_rank`: among the tokens of one rollout rank no scoring rank is named more than 64 times.
All inputs are finite; a program needn't handle non-finite values.
Results may differ from the reference program's by a relative error of at most 0.003.
The reference program's roundings to bfloat16 on the way count: a program that leaves them out, or rounds other values in their place, can miss the bound.
Values may be sent and summed in bfloat16 or wider, within the bound.
No kernel may reach another device: no remote copies, remote signals or barrier semaphores. Data moves between devices by JAX's collectives and lax.ppermute only.
A program may use at most 128 MiB of HBM per device.

```python
import math
import jax
import jax.numpy as jnp
import numpy as np
from jax import lax

D = 8192
QH = 64
KVH = 8
HD = 128
ROWS = 256
RESP_DEV = 4
MAXLEN = 128
CAP = 64
SLOTS = 512
TOKENS = 2048
N_FSDP = 8


def draw_queries(key, part):
    key = jax.random.fold_in(key, 7)
    first_key = jax.random.fold_in(key, 0)
    return jnp.clip(jax.random.normal(first_key, (TOKENS, QH * HD), jnp.float32), -6.0, 6.0).astype(jnp.bfloat16)


def block_levels(stream_key, dims, cuts, low, top_value):
    factor_of = 1.0
    for axis_at, parts in cuts:
        steps = jax.random.uniform(jax.random.fold_in(jax.random.fold_in(stream_key, 6), axis_at), (parts,), jnp.float32, low / len(cuts), top_value / len(cuts))
        factor_of = factor_of * jnp.repeat(jnp.exp(steps), dims[axis_at] // parts).reshape((-1,) + (1,) * (len(dims) - 1 - axis_at))
    return factor_of


def length_profile(number_of, total, bound, lean):
    weights = [(1 << 20) // math.isqrt(rank ** lean) + 1 for rank in range(2, number_of + 1)]
    surplus, holding = total - bound - (number_of - 1), [1] * (number_of - 1)
    while surplus > 0:
        movable = [i for i in range(number_of - 1) if holding[i] < bound]
        pool, budget = sum([weights[i] for i in movable]), surplus
        for i in movable:
            more = min(bound - holding[i], max(1, budget * weights[i] // pool), surplus)
            holding[i] = holding[i] + more
            surplus = surplus - more
    return np.array([bound] + holding)


def uneven_parts(key, number_of, total, bound, lean):
    if number_of == 2:
        one = jax.random.randint(key, (), max(1, total - bound), min(bound, total - 1) + 1)
        return jnp.stack([one, total - one])
    sizes = jnp.asarray(length_profile(number_of, total, bound, lean), jnp.int32)
    couples = (number_of - 1) // 2
    giver, sink = sizes[1:1 + 2 * couples:2], sizes[2:2 + 2 * couples:2]
    margin = jnp.minimum(giver - 1, bound - sink)
    passed = jax.random.randint(jax.random.fold_in(key, 1), (couples,), 0, 1 << 20) % (margin + 1)
    sizes = sizes.at[1:1 + 2 * couples:2].set(giver - passed).at[2:2 + 2 * couples:2].set(sink + passed)
    return sizes[jax.random.permutation(jax.random.fold_in(key, 2), number_of)]


def assign_block(rng, own, number, rows, number_of, top, limit, lean):
    order = jax.random.permutation(rng, number_of)
    packed, common = portions_of(number_of, rows * top, limit, lean, True), portions_of(number_of, rows * top, limit, lean, False)
    places = jnp.arange(number_of)

    def named(sizes, rotation):
        used = int((sizes > 0).sum())
        fixed = max(1, used // 4)
        shifted = fixed + (places - fixed + rotation * (used - fixed)) % max(1, number_of - fixed)
        return jnp.zeros((number_of,), jnp.int32).at[order[jnp.where(places < fixed, places, shifted)]].set(jnp.asarray(sizes, jnp.int32))

    sizes = jnp.where(number % 4 == 0, named(packed, number // 4), named(common, number - number // 4 - 1))
    mixed = jax.random.permutation(jax.random.fold_in(own, 3), number_of)
    donor, taker = mixed[0:number_of // 2 * 2:2], mixed[1:number_of // 2 * 2:2]
    slack = jnp.minimum(sizes[donor] - 1, limit - sizes[taker]) // 2
    slack = jnp.where((donor == order[0]) | (taker == order[0]) | (sizes[taker] == 0), 0, jnp.maximum(slack, 0))
    shifted = jax.random.randint(jax.random.fold_in(own, 4), (number_of // 2,), 0, 1 << 20) % (slack + 1)
    sizes = sizes.at[donor].add(-shifted).at[taker].add(shifted)
    members = jnp.searchsorted(jnp.cumsum(sizes), jnp.arange(rows * top), side="right").astype(jnp.int32)
    table = members.reshape(top, rows).T
    table = table[jax.random.permutation(jax.random.fold_in(own, 1), rows)]
    rotation = jax.random.randint(jax.random.fold_in(own, 2), (rows, 1), 0, top)
    return jnp.take_along_axis(table, (jnp.arange(top)[None, :] + rotation) % top, axis=1)


def portions_of(count, total, reach, slope, full):
    weights = [(1 << 20) // math.isqrt(rank ** slope) + 1 for rank in range(1, count + 1)]
    largest = reach if full else min(reach, max(-(-total // count), total * weights[0] // sum(weights)))
    least = 1 if total - largest >= count - 1 else 0
    given, surplus = [largest] + [least] * (count - 1), total - largest - least * (count - 1)
    while surplus > 0:
        free = [i for i in range(1, count) if given[i] < largest] or [i for i in range(1, count) if given[i] < reach]
        mass, budget = sum([weights[i] for i in free]), surplus
        for i in free:
            extra = min(reach - given[i], max(1, budget * weights[i] // mass), surplus)
            given[i] = given[i] + extra
            surplus = surplus - extra
    return np.array(given)


def gaussian(rng, extent, scale, reach, pieces=(), kind=jnp.bfloat16):
    values = jax.random.normal(rng, extent, jnp.float32) * scale
    if len(pieces) > 0:
        values = block_levels(rng, extent, pieces, -0.22, 0.18) * values
    return jnp.clip(values, min=-reach, max=reach).astype(kind)


def setup_inputs(seed: int = 0, part: int = 0) -> dict:
    key_of = jax.random.split(jax.random.key(seed), 8)
    part_splits = jax.random.split(jax.random.fold_in(key_of[7], part), 8)
    hidden = gaussian(part_splits[0], (TOKENS, D), 1.0, 6.0, ((0, 8), (1, 2)))
    queries = draw_queries(jax.random.fold_in(jax.random.fold_in(key_of[7], part), 71), part)
    lengths = jax.vmap(lambda own: uneven_parts(own, RESP_DEV, ROWS, MAXLEN, 2))(jax.random.split(part_splits[2], N_FSDP)).reshape((N_FSDP, RESP_DEV)).astype(jnp.int32)
    scoring_rank_keys = jax.random.split(jax.random.fold_in(part_splits[3], 1), TOKENS // ROWS)
    scoring_rank_turns = jax.random.permutation(jax.random.fold_in(part_splits[3], 3), TOKENS // ROWS)
    scoring_rank = jax.vmap(lambda own, number: assign_block(jax.random.fold_in(part_splits[3], 2), own, number, ROWS, N_FSDP, 1, CAP, 2))(scoring_rank_keys, scoring_rank_turns).reshape((TOKENS, 1))
    norm_gain = jnp.clip(1.0 + 0.18 * jax.random.normal(key_of[4], (D,), jnp.float32), 0.1, 1.9)
    kv_weight = gaussian(key_of[5], (D, KVH * 2 * HD), D ** -0.5, 0.0625, ((0, 8), (1, 2)))
    kv_bias = gaussian(key_of[6], (KVH * 2 * HD,), 0.5, 3.0, ((0, 2),), jnp.float32)
    return {"hidden": hidden, "queries": queries, "lengths": lengths, "scoring_rank": scoring_rank, "norm_gain": norm_gain, "kv_weight": kv_weight, "kv_bias": kv_bias}


EPSILON = 1e-06
THETA = 1000000.0

def rotate(values, position):
    width = values.shape[-1]
    half = width // 2
    freq = THETA ** (-jnp.arange(half, dtype=jnp.float32) * 2.0 / width)
    angles = position.astype(jnp.float32)[:, None] * freq[None, :]
    cosine = jnp.cos(angles)[:, None, :]
    sine = jnp.sin(angles)[:, None, :]
    first = values[..., :half]
    second = values[..., half:]
    return jnp.concatenate([first * cosine - second * sine, second * cosine + first * sine], -1)

def placement(lengths_row, count):
    ends = jnp.cumsum(lengths_row).astype(jnp.int32)
    starts = ends - lengths_row
    index = jnp.arange(count, dtype=jnp.int32)
    segment = lax.optimization_barrier(jnp.sum((index[:, None] >= ends[None, :]).astype(jnp.int32), 1))
    onehot = segment[:, None] == jnp.arange(lengths_row.shape[0], dtype=jnp.int32)[None, :]
    offset = lax.optimization_barrier(jnp.sum(jnp.where(onehot, starts[None, :], 0), 1)).astype(jnp.int32)
    return (segment, index - offset)

def attend_block(query_rows, keyval, lengths_row):
    count = query_rows.shape[0]
    segment, position = placement(lengths_row, count)
    keyval_heads = keyval.reshape(count, KVH, 2, HD)
    keys_rot = rotate(keyval_heads[:, :, 0].astype(jnp.float32), position).astype(jnp.bfloat16)
    values = keyval_heads[:, :, 1]
    group = QH // KVH
    queries_rot = rotate(query_rows.reshape(count, QH, HD).astype(jnp.float32), position).astype(jnp.bfloat16)
    queries_rot = queries_rot.reshape(count, KVH, group, HD)
    scores = jnp.einsum('qhgd,khd->hgqk', queries_rot.astype(jnp.float32), keys_rot.astype(jnp.float32)) * HD ** (-0.5)
    index = jnp.arange(count)
    allowed = (segment[:, None] == segment[None, :]) & (index[None, :] <= index[:, None])
    masked = jnp.where(allowed, scores, jnp.float32(-1e+30))
    top = lax.optimization_barrier(jnp.max(masked, -1, keepdims=True))
    weights = jnp.where(allowed, jnp.exp(masked - top), jnp.float32(0.0))
    probs = (weights / lax.optimization_barrier(jnp.sum(weights, -1, keepdims=True))).astype(jnp.bfloat16)
    output = jnp.einsum('hgqk,khd->qhgd', probs.astype(jnp.float32), values.astype(jnp.float32))
    return output.astype(jnp.bfloat16).reshape(count, QH * HD)

def reference(hidden, queries, lengths, scoring_rank, norm_gain, kv_weight, kv_bias):
    hidden_f = hidden.astype(jnp.float32)
    inverse_rms = lax.rsqrt(lax.optimization_barrier(jnp.mean(hidden_f * hidden_f, -1)) + EPSILON)
    normed = (hidden_f * inverse_rms[:, None] * norm_gain[None, :]).astype(jnp.bfloat16)
    keyval = (jnp.dot(normed, kv_weight, preferred_element_type=jnp.float32) + kv_bias[None, :]).astype(jnp.bfloat16)
    dest = scoring_rank[:, 0].reshape(N_FSDP, ROWS)
    onehot = (dest[:, :, None] == jnp.arange(N_FSDP, dtype=jnp.int32)[None, None, :]).astype(jnp.int32)
    before = jnp.cumsum(onehot, 1) - onehot
    slot = lax.optimization_barrier(jnp.sum(before * onehot, 2)).astype(jnp.int32)
    block = jnp.arange(N_FSDP, dtype=jnp.int32)[:, None]
    target = ((dest * N_FSDP + block) * CAP + slot).reshape(-1).astype(jnp.int32)
    base = jnp.broadcast_to(kv_bias.astype(jnp.bfloat16)[None, :], (N_FSDP * SLOTS, KVH * 2 * HD))
    scored_rows = base.at[target].set(keyval)
    blocks = (queries.reshape(N_FSDP, ROWS, QH * HD), keyval.reshape(N_FSDP, ROWS, KVH * 2 * HD), lengths)
    attended = lax.map(lambda item: attend_block(item[0], item[1], item[2]), blocks)
    return (attended.reshape(N_FSDP * ROWS, QH * HD), scored_rows)
```

```python
import functools

import jax
import jax.numpy as jnp
from jax import lax
from jax.experimental import pallas as pl
from jax.experimental.pallas import tpu as pltpu
from jax.sharding import PartitionSpec as P

HD = 128
EPSILON = 1e-06
THETA = 1000000.0
VMEM = pl.BlockSpec(memory_space=pltpu.VMEM)
SMEM = pl.BlockSpec(memory_space=pltpu.SMEM)
ANY = pl.BlockSpec(memory_space=pl.ANY)
PARAMS = pltpu.CompilerParams(vmem_limit_bytes=24 * 1024 * 1024)


def cost(flops, nbytes):
    return pl.CostEstimate(flops=flops, bytes_accessed=nbytes, transcendentals=0)


def norm_kernel(place, hidden, inverse, gain, *outs, slices, piece):
    for k, out in enumerate(outs):
        x = place[0] ^ (k & 1)
        y = place[1] ^ (k >> 1)
        for i in range(slices):
            start = pl.multiple_of((i * 4 + x * 2 + y) * piece, piece)
            cols = pl.ds(start, piece)
            values = hidden[:, cols].astype(jnp.float32) * inverse[...] * gain[:, cols]
            out[:, i * piece : (i + 1) * piece] = values.astype(jnp.bfloat16)


def matmul_kernel(place, *refs, count, piece, width):
    own, peer = refs[:4], refs[4:8]
    blocks = refs[8 : 8 + count]
    outs = refs[8 + count : 12 + count]
    weights = refs[12 + count]
    z, core = place[2], place[3]
    for s, block in enumerate(blocks):
        at = lax.rem(z - s + count, count)
        weights[pl.ds(pl.multiple_of(at * piece, piece), piece), :] = block[...]
    half = count // 2 * piece
    mine = weights[pl.ds(pl.multiple_of(core * half, half), half), :]
    others = weights[pl.ds(pl.multiple_of((1 - core) * half, half), half), :]
    for k in range(4):
        outs[k][...] = jnp.dot(
            own[k][...], mine, preferred_element_type=jnp.float32
        ) + jnp.dot(peer[k][...], others, preferred_element_type=jnp.float32)


def rows_kernel(a, b, c, d, bias, onehot, used, keyval, outgoing):
    summed = (a[...] + b[...]) + (c[...] + d[...])
    rows = (summed + bias[...]).astype(jnp.bfloat16)
    keyval[...] = rows
    moved = jnp.dot(onehot[...], rows, preferred_element_type=jnp.float32)
    empty = bias[...].astype(jnp.bfloat16).astype(jnp.float32)
    outgoing[...] = jnp.where(used[...] > 0, moved, empty).astype(jnp.bfloat16)


def turn(values, cosine, sine):
    half = HD // 2
    turned = jnp.concatenate([values[:, half:], values[:, :half]], -1)
    return values * cosine + turned * sine


def rotate_kernel(queries, cosine, sine, out):
    for h in range(queries.shape[1] // HD):
        cols = slice(h * HD, (h + 1) * HD)
        values = queries[:, cols].astype(jnp.float32)
        out[:, cols] = turn(values, cosine[...], sine[...]).astype(jnp.bfloat16)


def attend_kernel(queries, keyval, cosine, sine, mask, *rest, heads):
    out = rest[-1]
    count = keyval.shape[0]
    half = count // 2
    keys = turn(keyval[:, :HD].astype(jnp.float32), cosine[...], sine[...])
    keys = keys.astype(jnp.bfloat16)
    values = keyval[:, HD:]
    for h in range(heads):
        cols = slice(h * HD, (h + 1) * HD)
        for first, reach in ((0, half), (half, count)):
            rows = slice(first, first + half)
            scores = lax.dot_general(
                queries[rows, cols],
                keys[:reach],
                (((1,), (1,)), ((), ())),
                preferred_element_type=jnp.float32,
            )
            masked = scores * HD ** (-0.5) + mask[rows, :reach]
            top = jnp.max(masked, -1, keepdims=True)
            weights = jnp.exp(masked - top)
            total = jnp.sum(weights, -1, keepdims=True)
            probs = (weights * (1.0 / total)).astype(jnp.bfloat16)
            out[rows, cols] = jnp.dot(
                probs, values[:reach], preferred_element_type=jnp.float32
            ).astype(jnp.bfloat16)


def shards(hidden, queries, lengths, scoring_rank, norm_gain, kv_weight, kv_bias):
    ranks = lax.axis_size("fsdp")
    steps = ranks // 2
    count, features = hidden.shape
    width = features * lax.axis_size("tp")
    depth, columns = kv_weight.shape
    piece = depth // 2
    heads = columns // (2 * HD)
    group = queries.shape[1] // HD // heads
    capacity = 2 * count // ranks
    slots = capacity * ranks

    f = lax.axis_index("fsdp")
    y = lax.axis_index("groups")
    core = lax.axis_index("tp")
    x, z = lax.rem(f, 2), lax.div(f, 2)
    place = jnp.stack([x, y, z, core]).astype(jnp.int32)

    right = [(i, (i + 2) % ranks) for i in range(ranks)]
    left = [(i, (i - 2) % ranks) for i in range(ranks)]
    flip_x = [(i, i ^ 1) for i in range(ranks)]
    flip_y = [(0, 1), (1, 0)]
    flip_xy = [(g * ranks + i, (1 - g) * ranks + (i ^ 1)) for g in range(2) for i in range(ranks)]

    def to_chip(k, array):
        if k == 1:
            return lax.ppermute(array, "fsdp", flip_x)
        if k == 2:
            return lax.ppermute(array, "groups", flip_y)
        return lax.ppermute(array, ("groups", "fsdp"), flip_xy)

    half_rows = lax.dynamic_slice(kv_weight, (y * piece, 0), (piece, columns))
    gathered = []
    held = None
    for j in range(heads):
        block = half_rows[:, j * 2 * HD : (j + 1) * 2 * HD]
        if held is not None:
            block, _ = lax.optimization_barrier((block, held))
        ups, downs = [block], [block]
        for _ in range(steps // 2):
            ups.append(lax.ppermute(ups[-1], "fsdp", right))
        for _ in range((steps - 1) // 2):
            downs.append(lax.ppermute(downs[-1], "fsdp", left))
        gathered.append(ups + downs[:0:-1])
        held = (ups[1], downs[1])

    hidden_f = hidden.astype(jnp.float32)
    squares = jnp.sum(hidden_f * hidden_f, -1, keepdims=True)
    squares = squares + lax.ppermute(squares, "tp", flip_y)
    inverse_rms = lax.rsqrt(squares / width + EPSILON)
    slices = features // (4 * piece)
    if piece % HD == 0:
        normed = pl.pallas_call(
            functools.partial(norm_kernel, slices=slices, piece=piece),
            out_shape=[jax.ShapeDtypeStruct((count, features // 4), jnp.bfloat16)] * 4,
            in_specs=[SMEM] + [VMEM] * 3,
            out_specs=[VMEM] * 4,
            compiler_params=PARAMS,
            cost_estimate=cost(3 * count * features, 4 * count * features),
            name="norm",
        )(place, hidden, inverse_rms, norm_gain[None, :])
    else:
        whole = (hidden_f * inverse_rms * norm_gain[None, :]).astype(jnp.bfloat16)
        whole = whole.reshape(count, slices, 2, 2, piece)
        normed = []
        for k in range(4):
            part = lax.dynamic_index_in_dim(whole, x ^ (k & 1), 2, False)
            part = lax.dynamic_index_in_dim(part, y ^ (k >> 1), 2, False)
            normed.append(part.reshape(count, features // 4))
    own = [normed[0]] + [to_chip(k, normed[k]) for k in (1, 2, 3)]
    peer = [lax.ppermute(block, "tp", flip_y) for block in own]

    dest = scoring_rank[:, 0]
    index = jnp.arange(count, dtype=jnp.int32)
    earlier = (dest[:, None] == dest[None, :]) & (index[:, None] < index[None, :])
    slot = jnp.sum(earlier.astype(jnp.int32), 0)
    target = dest * capacity + slot
    hits = jnp.arange(slots, dtype=jnp.int32)[:, None] == target[None, :]
    onehot = hits.astype(jnp.bfloat16)
    used = jnp.any(hits, 1, keepdims=True).astype(jnp.float32)

    row = lengths[0]
    ends = jnp.cumsum(row)
    starts = ends - row
    within = (index[:, None] >= starts[None, :]) & (index[:, None] < ends[None, :])
    start = jnp.sum(jnp.where(within, starts[None, :], 0), 1)
    position = index - start
    freq = THETA ** (-jnp.arange(HD // 2, dtype=jnp.float32) * 2.0 / HD)
    angles = position.astype(jnp.float32)[:, None] * freq[None, :]
    cosine, sine = jnp.cos(angles), jnp.sin(angles)
    cosine = jnp.concatenate([cosine, cosine], 1)
    sine = jnp.concatenate([-sine, sine], 1)
    allowed = (index[None, :] >= start[:, None]) & (index[None, :] <= index[:, None])
    mask = jnp.where(allowed, jnp.float32(0.0), jnp.float32(-1e30))
    turned = pl.pallas_call(
        rotate_kernel,
        out_shape=jax.ShapeDtypeStruct(queries.shape, jnp.bfloat16),
        in_specs=[VMEM] * 3,
        out_specs=VMEM,
        compiler_params=PARAMS,
        cost_estimate=cost(4 * count * queries.shape[1], 4 * count * queries.shape[1]),
        name="rotate",
    )(queries, cosine, sine)

    attended = None
    received = []
    bias = kv_bias[None, :]
    for j in range(heads):
        cols = slice(j * 2 * HD, (j + 1) * 2 * HD)
        parts = pl.pallas_call(
            functools.partial(matmul_kernel, count=steps, piece=piece, width=2 * HD),
            out_shape=[jax.ShapeDtypeStruct((count, 2 * HD), jnp.float32)] * 4,
            in_specs=[SMEM] + [VMEM] * (8 + steps),
            out_specs=[VMEM] * 4,
            scratch_shapes=[pltpu.VMEM((steps * piece, 2 * HD), jnp.bfloat16)],
            compiler_params=PARAMS,
            cost_estimate=cost(2 * 4 * count * steps * piece * 2 * HD, 6 << 20),
            name="project",
        )(place, *own, *peer, *gathered[j])
        sums = [parts[0]] + [to_chip(k, parts[k]) for k in (1, 2, 3)]
        keyval, outgoing = pl.pallas_call(
            rows_kernel,
            out_shape=[
                jax.ShapeDtypeStruct((count, 2 * HD), jnp.bfloat16),
                jax.ShapeDtypeStruct((slots, 2 * HD), jnp.bfloat16),
            ],
            in_specs=[VMEM] * 7,
            out_specs=[VMEM] * 2,
            compiler_params=PARAMS,
            cost_estimate=cost(2 * slots * count * 2 * HD, 2 << 20),
            name="rows",
        )(*sums, bias[:, cols], onehot, used)
        received.append(
            lax.all_to_all(outgoing, "fsdp", split_axis=0, concat_axis=0, tiled=True)
        )
        before = [] if attended is None else [attended]
        attended = pl.pallas_call(
            functools.partial(attend_kernel, heads=group),
            out_shape=jax.ShapeDtypeStruct(queries.shape, jnp.bfloat16),
            grid=(1,),
            in_specs=[
                pl.BlockSpec((count, group * HD), lambda i, j=j: (0, j)),
                pl.BlockSpec((count, 2 * HD), lambda i: (0, 0)),
                pl.BlockSpec((count, HD), lambda i: (0, 0)),
                pl.BlockSpec((count, HD), lambda i: (0, 0)),
                pl.BlockSpec((count, count), lambda i: (0, 0)),
            ]
            + [ANY] * len(before),
            out_specs=pl.BlockSpec((count, group * HD), lambda i, j=j: (0, j)),
            input_output_aliases={5: 0} if before else {},
            compiler_params=PARAMS,
            cost_estimate=cost(4 * group * count * count * HD, 2 << 20),
            name="attend",
        )(turned, keyval, cosine, sine, mask, *before)
    scored_rows = jnp.concatenate(received, 1)
    return (attended, scored_rows)


def solution(mesh):
    placed = (
        P(("groups", "fsdp"), "tp"),
        P(("groups", "fsdp"), "tp"),
        P(("groups", "fsdp"), None),
        P(("groups", "fsdp"), None),
        P("tp"),
        P("fsdp", "tp"),
        P("tp"),
    )
    return jax.shard_map(
        shards,
        mesh=mesh,
        in_specs=placed,
        out_specs=(P(("groups", "fsdp"), "tp"), P(("groups", "fsdp"), "tp")),
        check_vma=False,
    )
```

```python
import functools

import jax
import jax.numpy as jnp
from jax import lax
from jax.experimental import pallas as pl
from jax.experimental.pallas import tpu as pltpu
from jax.sharding import PartitionSpec as P

HD = 128
EPSILON = 1e-06
THETA = 1000000.0
VMEM = pl.BlockSpec(memory_space=pltpu.VMEM)
SMEM = pl.BlockSpec(memory_space=pltpu.SMEM)
FULL = pltpu.CompilerParams(vmem_limit_bytes=56 * 1024 * 1024)
ANY = pl.BlockSpec(memory_space=pl.ANY)
PARAMS = pltpu.CompilerParams(vmem_limit_bytes=16 * 1024 * 1024)


def after(value, *others):
    return lax.optimization_barrier((value, *others))[0]


def cost(flops, nbytes):
    return pl.CostEstimate(flops=flops, bytes_accessed=nbytes, transcendentals=0)


def squares_kernel(hidden, out):
    values = hidden[...].astype(jnp.float32)
    out[...] = jnp.sum(values * values, -1, keepdims=True)


def norm_kernel(place, hidden, inverse, gain, *outs, slices, piece):
    for k, out in enumerate(outs):
        x = place[0] ^ (k & 1)
        y = place[1] ^ (k >> 1)
        for i in range(slices):
            start = pl.multiple_of((i * 4 + x * 2 + y) * piece, piece)
            cols = pl.ds(start, piece)
            values = hidden[:, cols].astype(jnp.float32) * inverse[...] * gain[:, cols]
            out[:, i * piece : (i + 1) * piece] = values.astype(jnp.bfloat16)


def matmul_kernel(place, *refs, count, piece):
    rows = refs[:8]
    blocks = refs[8 : 8 + count]
    outs = refs[8 + count : -4]
    held, weights, row_sems, sems = refs[-4:]
    z, core = place[2], place[3]
    copies = []
    for s, block in enumerate(blocks):
        at = pl.multiple_of(lax.rem(z - s + count, count) * piece, piece)
        copies.append(pltpu.make_async_copy(block, weights.at[pl.ds(at, piece), :], sems.at[s]))
    loads = [pltpu.make_async_copy(rows[i], held.at[i], row_sems.at[i]) for i in range(8)]
    for copy in copies:
        copy.start()
    for k in range(4):
        loads[k].start()
        loads[4 + k].start()
    for copy in copies:
        copy.wait()
    half = count // 2 * piece
    mine = pl.ds(pl.multiple_of(core * half, half), half)
    others = pl.ds(pl.multiple_of((1 - core) * half, half), half)
    middle = weights.shape[1] // 2
    for k in range(4):
        loads[k].wait()
        loads[4 + k].wait()
        total = jnp.dot(
            held[k], weights[mine, :], preferred_element_type=jnp.float32
        ) + jnp.dot(held[4 + k], weights[others, :], preferred_element_type=jnp.float32)
        outs[k & 1][k >> 1] = total[:, :middle]
        outs[2 + (k >> 1)][k & 1] = total[:, middle:]


def fold_kernel(kept_a, came_a, kept_b, came_b, mine, next_a, next_b):
    middle = kept_a.shape[2]
    mine[:, :middle] = kept_a[0] + came_a[0]
    mine[:, middle:] = kept_b[0] + came_b[0]
    next_a[...] = kept_a[1] + came_a[1]
    next_b[...] = kept_b[1] + came_b[1]


def rows_kernel(bias, target, mine, came_a, came_b, *refs, earlier):
    before = refs[:earlier]
    keyval = refs[earlier]
    wide = keyval.shape[1]
    at = bias.shape[1] - wide
    summed = mine[...] + jnp.concatenate([came_a[...], came_b[...]], 1)
    rows = (summed + bias[:, at:]).astype(jnp.bfloat16)
    keyval[...] = rows
    if len(refs) == earlier + 1:
        return
    outgoing = refs[-1]
    slots, count = outgoing.shape[0], rows.shape[0]
    hits = lax.broadcasted_iota(jnp.int32, (slots, count), 0) == target[...]
    onehot = hits.astype(jnp.float32)
    used = jnp.sum(onehot, 1, keepdims=True)
    onehot = onehot.astype(jnp.bfloat16)
    begin = 0
    for block in [ref[...] for ref in before] + [rows]:
        cols = slice(begin, begin + block.shape[1])
        moved = jnp.dot(onehot, block, preferred_element_type=jnp.float32)
        empty = bias[:, cols].astype(jnp.bfloat16).astype(jnp.float32)
        outgoing[:, cols] = jnp.where(used > 0, moved, empty).astype(jnp.bfloat16)
        begin += block.shape[1]


def turn(values, cosine, sine):
    half = HD // 2
    turned = jnp.concatenate([values[:, half:], values[:, :half]], -1)
    return values * cosine + turned * sine


def rotate_kernel(queries, cosine, sine, out):
    for h in range(queries.shape[1] // HD):
        cols = slice(h * HD, (h + 1) * HD)
        values = queries[:, cols].astype(jnp.float32)
        out[:, cols] = turn(values, cosine[...], sine[...]).astype(jnp.bfloat16)


def attend_kernel(queries, keyval, cosine, sine, start, *rest, group):
    out = rest[-1]
    count = keyval.shape[0]
    token = lax.broadcasted_iota(jnp.int32, (count, count), 0)
    other = lax.broadcasted_iota(jnp.int32, (count, count), 1)
    allowed = (other >= start[...]) & (other <= token)
    mask = jnp.where(allowed, jnp.float32(0.0), jnp.float32(-1e30))
    half = count // 2
    keys = turn(keyval[:, :HD].astype(jnp.float32), cosine[...], sine[...])
    keys = keys.astype(jnp.bfloat16)
    values = keyval[:, HD:]
    for first, reach in ((0, half), (half, count)):
        rows = slice(first, first + half)
        stacked = jnp.concatenate(
            [queries[rows, h * HD : (h + 1) * HD] for h in range(group)], 0
        )
        scores = lax.dot_general(
            stacked,
            keys[:reach],
            (((1,), (1,)), ((), ())),
            preferred_element_type=jnp.float32,
        )
        masked = scores.reshape(group, half, reach) * HD ** (-0.5) + mask[rows, :reach]
        top = jnp.max(masked, -1, keepdims=True)
        weights = jnp.exp(masked - top)
        total = jnp.sum(weights, -1, keepdims=True)
        probs = (weights * (1.0 / total)).astype(jnp.bfloat16)
        mixed = jnp.dot(
            probs.reshape(group * half, reach),
            values[:reach],
            preferred_element_type=jnp.float32,
        ).astype(jnp.bfloat16)
        for h in range(group):
            out[rows, h * HD : (h + 1) * HD] = mixed[h * half : (h + 1) * half]


def chunks_of(heads):
    sizes = [heads // 2, heads - heads // 2]
    return [(sum(sizes[:i]), size) for i, size in enumerate(sizes) if size]


def shards(hidden, queries, lengths, scoring_rank, norm_gain, kv_weight, kv_bias):
    ranks = lax.axis_size("fz") * 2
    steps = ranks // 2
    count, features = hidden.shape
    width = features * lax.axis_size("tp")
    depth, columns = kv_weight.shape
    piece = depth // 2
    heads = columns // (2 * HD)
    group = queries.shape[1] // HD // heads
    capacity = 2 * count // ranks
    slots = capacity * ranks

    y = lax.axis_index("groups")
    core = lax.axis_index("tp")
    x, z = lax.axis_index("fx"), lax.axis_index("fz")
    place = jnp.stack([x, y, z, core]).astype(jnp.int32)

    right = [(i, (i + 1) % steps) for i in range(steps)]
    left = [(i, (i - 1) % steps) for i in range(steps)]
    flip = [(0, 1), (1, 0)]
    flip_both = [(i, 3 - i) for i in range(4)]

    def to_chip(k, array):
        if k == 1:
            return lax.ppermute(array, "fx", flip)
        if k == 2:
            return lax.ppermute(array, "groups", flip)
        return lax.ppermute(array, ("groups", "fx"), flip_both)

    hidden_f = hidden.astype(jnp.float32)
    squares = pl.pallas_call(
        squares_kernel,
        out_shape=jax.ShapeDtypeStruct((count, 1), jnp.float32),
        in_specs=[VMEM],
        out_specs=VMEM,
        compiler_params=PARAMS,
        cost_estimate=cost(2 * count * features, 1 << 20),
        name="squares",
    )(hidden)

    chunks = chunks_of(heads)
    gathered = []

    def gather(first, number, *waits):
        cut = (piece, number * 2 * HD)
        if not gathered:
            source, end = kv_weight, squares
        else:
            source, end = after(kv_weight, gathered[-1][-1], *waits), gathered[-1][steps // 2]
        block = lax.dynamic_slice(source, (y * piece, first * 2 * HD), cut)
        ups, downs = [block], [after(block, end)]
        for _ in range(steps // 2):
            ups.append(lax.ppermute(ups[-1], "fz", right))
        for _ in range((steps - 1) // 2):
            downs.append(lax.ppermute(downs[-1], "fz", left))
        gathered.append(ups + downs[:0:-1])

    for chunk in chunks:
        gather(*chunk)

    squares = squares + lax.ppermute(squares, "tp", flip)
    inverse_rms = lax.rsqrt(squares / width + EPSILON)
    slices = features // (4 * piece)
    if piece % HD == 0:
        normed = pl.pallas_call(
            functools.partial(norm_kernel, slices=slices, piece=piece),
            out_shape=[jax.ShapeDtypeStruct((count, features // 4), jnp.bfloat16)] * 4,
            in_specs=[SMEM] + [VMEM] * 3,
            out_specs=[VMEM] * 4,
            compiler_params=PARAMS,
            cost_estimate=cost(3 * count * features, 4 * count * features),
            name="norm",
        )(place, hidden, inverse_rms, norm_gain[None, :])
    else:
        whole = (hidden_f * inverse_rms * norm_gain[None, :]).astype(jnp.bfloat16)
        whole = whole.reshape(count, slices, 2, 2, piece)
        normed = []
        for k in range(4):
            part = lax.dynamic_index_in_dim(whole, x ^ (k & 1), 2, False)
            part = lax.dynamic_index_in_dim(part, y ^ (k >> 1), 2, False)
            normed.append(part.reshape(count, features // 4))
    own = [normed[0]] + [to_chip(k, normed[k]) for k in (1, 2, 3)]
    late = [after(own[0], own[2]), after(own[1], gathered[0][1])]
    peer = [lax.ppermute(block, "tp", flip) for block in late + own[2:]]

    dest = scoring_rank[:, 0]
    index = jnp.arange(count, dtype=jnp.int32)
    earlier = (dest[:, None] == dest[None, :]) & (index[:, None] < index[None, :])
    slot = jnp.sum(earlier.astype(jnp.int32), 0)
    target = dest * capacity + slot
    row = lengths[0]
    ends = jnp.cumsum(row)
    starts = ends - row
    within = (index[:, None] >= starts[None, :]) & (index[:, None] < ends[None, :])
    start = jnp.sum(jnp.where(within, starts[None, :], 0), 1)
    position = index - start
    freq = THETA ** (-jnp.arange(HD // 2, dtype=jnp.float32) * 2.0 / HD)
    angles = position.astype(jnp.float32)[:, None] * freq[None, :]
    cosine, sine = jnp.cos(angles), jnp.sin(angles)
    cosine = jnp.concatenate([cosine, cosine], 1)
    sine = jnp.concatenate([-sine, sine], 1)
    turned = pl.pallas_call(
        rotate_kernel,
        out_shape=jax.ShapeDtypeStruct(queries.shape, jnp.bfloat16),
        in_specs=[VMEM] * 3,
        out_specs=VMEM,
        compiler_params=PARAMS,
        cost_estimate=cost(4 * count * queries.shape[1], 4 * count * queries.shape[1]),
        name="rotate",
    )(queries, cosine, sine)

    bias = kv_bias[None, :]
    attended = None
    waiting, sent = [], 0
    scored_rows = None
    last = (turned, target, start)
    for n, (first, number) in enumerate(chunks):
        wide = number * 2 * HD
        middle = wide // 2
        where = after(place, *last)
        kept_a, sent_a, kept_b, sent_b = pl.pallas_call(
            functools.partial(matmul_kernel, count=steps, piece=piece),
            out_shape=[jax.ShapeDtypeStruct((2, count, middle), jnp.float32)] * 4,
            in_specs=[SMEM] + [ANY] * (8 + steps),
            out_specs=[VMEM] * 4,
            scratch_shapes=[
                pltpu.VMEM((8, count, steps * piece // 2), jnp.bfloat16),
                pltpu.VMEM((steps * piece, wide), jnp.bfloat16),
                pltpu.SemaphoreType.DMA((8,)),
                pltpu.SemaphoreType.DMA((steps,)),
            ],
            compiler_params=FULL,
            cost_estimate=cost(2 * 4 * count * steps * piece * wide, 1 << 20),
            name="project",
        )(where, *own, *peer, *gathered[n])
        came_a, came_b = to_chip(1, sent_a), to_chip(2, sent_b)
        if n + 1 < len(chunks):
            came_a = after(came_a, gathered[n + 1][1])
        mine, next_a, next_b = pl.pallas_call(
            fold_kernel,
            out_shape=[jax.ShapeDtypeStruct((count, wide), jnp.float32)]
            + [jax.ShapeDtypeStruct((count, middle), jnp.float32)] * 2,
            in_specs=[VMEM] * 4,
            out_specs=[VMEM] * 3,
            compiler_params=PARAMS,
            cost_estimate=cost(2 * count * wide, 1 << 18),
            name="fold",
        )(kept_a, came_a, kept_b, came_b)
        share = [mine, to_chip(2, next_a), to_chip(1, next_b)]
        end = first * 2 * HD + wide
        added = bias[:, sent:end]
        if n + 1 < len(chunks):
            added = after(added, gathered[n + 1][-1])
        if attended is not None:
            added, attended = lax.optimization_barrier((added, attended))
        routed = True
        earlier = waiting if routed else []
        outs = [jax.ShapeDtypeStruct((count, wide), jnp.bfloat16)]
        if routed:
            outs.append(jax.ShapeDtypeStruct((slots, end - sent), jnp.bfloat16))
        keyval, *outgoing = pl.pallas_call(
            functools.partial(rows_kernel, earlier=len(earlier)),
            out_shape=outs,
            in_specs=[VMEM] * (5 + len(earlier)),
            out_specs=[VMEM] * len(outs),
            compiler_params=PARAMS,
            cost_estimate=cost(2 * slots * count * wide, 1 << 20),
            name="rows",
        )(added, target[None, :], *share, *earlier)
        last = (keyval,)
        waiting.append(keyval)
        if routed:
            received = lax.all_to_all(outgoing[0], ("fz", "fx"), split_axis=0, concat_axis=0, tiled=True)
            columns_at = pl.BlockSpec((slots, end - sent), lambda i, at=sent // (end - sent): (0, at))
            before = [] if scored_rows is None else [scored_rows]
            scored_rows = pl.pallas_call(
                lambda *refs: refs[-1].__setitem__(Ellipsis, refs[0][...]),
                out_shape=jax.ShapeDtypeStruct((slots, columns), jnp.bfloat16),
                grid=(1,),
                in_specs=[pl.BlockSpec((slots, end - sent), lambda i: (0, 0))] + [ANY] * len(before),
                out_specs=columns_at,
                input_output_aliases={1: 0} if before else {},
                compiler_params=PARAMS,
                cost_estimate=cost(1, 1 << 19),
                name="store",
            )(received, *before)
            waiting, sent = [], end
        before = [] if attended is None else [attended]
        attended = pl.pallas_call(
            functools.partial(attend_kernel, group=group),
            out_shape=jax.ShapeDtypeStruct(queries.shape, jnp.bfloat16),
            grid=(number,),
            in_specs=[
                pl.BlockSpec((count, group * HD), lambda i, at=first: (0, at + i)),
                pl.BlockSpec((count, 2 * HD), lambda i: (0, i)),
                pl.BlockSpec((count, HD), lambda i: (0, 0)),
                pl.BlockSpec((count, HD), lambda i: (0, 0)),
                pl.BlockSpec((count, 1), lambda i: (0, 0)),
            ]
            + [ANY] * len(before),
            out_specs=pl.BlockSpec((count, group * HD), lambda i, at=first: (0, at + i)),
            input_output_aliases={5: 0} if before else {},
            compiler_params=PARAMS,
            cost_estimate=cost(4 * number * group * count * count * HD, 1 << 20),
            name="attend",
        )(turned, keyval, cosine, sine, start[:, None], *before)
    return (attended, scored_rows)


def solution(mesh):
    groups, ranks, cores = (mesh.shape[name] for name in ("groups", "fsdp", "tp"))
    devices = mesh.devices.reshape(groups, ranks // 2, 2, cores)
    paired = jax.sharding.Mesh(devices, ("groups", "fz", "fx", "tp"))
    rows = ("groups", "fz", "fx")
    placed = (
        P(rows, "tp"),
        P(rows, "tp"),
        P(rows, None),
        P(rows, None),
        P("tp"),
        P(("fz", "fx"), "tp"),
        P("tp"),
    )
    return jax.shard_map(
        shards,
        mesh=paired,
        in_specs=placed,
        out_specs=(P(rows, "tp"), P(rows, "tp")),
        check_vma=False,
    )
```

```python
import functools

import jax
import jax.numpy as jnp
from jax import lax
from jax.experimental import pallas as pl
from jax.experimental.pallas import tpu as pltpu
from jax.sharding import PartitionSpec as P

HD = 128
EPSILON = 1e-06
THETA = 1000000.0
VMEM = pl.BlockSpec(memory_space=pltpu.VMEM)
SMEM = pl.BlockSpec(memory_space=pltpu.SMEM)
FULL = pltpu.CompilerParams(vmem_limit_bytes=40 * 1024 * 1024)
ANY = pl.BlockSpec(memory_space=pl.ANY)
PARAMS = pltpu.CompilerParams(vmem_limit_bytes=16 * 1024 * 1024)


def after(value, *others):
    return lax.optimization_barrier((value, *others))[0]


def cost(flops, nbytes):
    return pl.CostEstimate(flops=flops, bytes_accessed=nbytes, transcendentals=0)


def squares_kernel(hidden, out):
    values = hidden[...].astype(jnp.float32)
    out[...] = jnp.sum(values * values, -1, keepdims=True)


def norm_kernel(place, hidden, inverse, gain, *outs, slices, piece):
    for k, out in enumerate(outs):
        x = place[0] ^ (k & 1)
        y = place[1] ^ (k >> 1)
        for i in range(slices):
            start = pl.multiple_of((i * 4 + x * 2 + y) * piece, piece)
            cols = pl.ds(start, piece)
            values = hidden[:, cols].astype(jnp.float32) * inverse[...] * gain[:, cols]
            out[:, i * piece : (i + 1) * piece] = values.astype(jnp.bfloat16)


def matmul_kernel(place, *refs, count, piece):
    rows = refs[:8]
    blocks = refs[8 : 8 + count]
    outs = refs[8 + count : -4]
    held, weights, row_sems, sems = refs[-4:]
    z, core = place[2], place[3]
    copies = []
    for s, block in enumerate(blocks):
        at = pl.multiple_of(lax.rem(z - s + count, count) * piece, piece)
        copies.append(pltpu.make_async_copy(block, weights.at[pl.ds(at, piece), :], sems.at[s]))
    loads = [pltpu.make_async_copy(rows[i], held.at[i], row_sems.at[i]) for i in range(8)]
    for copy in copies:
        copy.start()
    for k in range(4):
        loads[k].start()
        loads[4 + k].start()
    for copy in copies:
        copy.wait()
    half = count // 2 * piece
    mine = pl.ds(pl.multiple_of(core * half, half), half)
    others = pl.ds(pl.multiple_of((1 - core) * half, half), half)
    middle = weights.shape[1] // 2
    for k in range(4):
        loads[k].wait()
        loads[4 + k].wait()
        total = jnp.dot(
            held[k], weights[mine, :], preferred_element_type=jnp.float32
        ) + jnp.dot(held[4 + k], weights[others, :], preferred_element_type=jnp.float32)
        outs[k & 1][k >> 1] = total[:, :middle]
        outs[2 + (k >> 1)][k & 1] = total[:, middle:]


def early_kernel(place, *refs, count, piece, order):
    rows, blocks, outs, later = refs[:8], refs[8:-9], refs[-9:-5], refs[-5]
    held, weights, row_sems, sems = refs[-4:]
    z, core = place[2], place[3]
    copies = [
        pltpu.make_async_copy(block, weights.at[i], sems.at[i]) for i, block in enumerate(blocks)
    ]
    loads = [pltpu.make_async_copy(rows[i], held.at[i], row_sems.at[i]) for i in range(8)]
    for copy in copies:
        copy.start()
    for k in range(4):
        loads[k].start()
        loads[4 + k].start()
    for copy in copies:
        copy.wait()
    half = count // 2
    middle = weights.shape[2] // 2

    def features(k, s):
        at = lax.rem(z - s + count, count)
        side = jnp.where(lax.div(at, half) == core, 0, 4)
        cols = pl.ds(pl.multiple_of(lax.rem(at, half) * piece, piece), piece)
        return held[side + k, :, cols]

    for k in range(4):
        loads[k].wait()
        loads[4 + k].wait()
        later[k] = features(k, count // 2)
        total = None
        for i, s in enumerate(order):
            part = jnp.dot(features(k, s), weights[i], preferred_element_type=jnp.float32)
            total = part if total is None else total + part
        outs[k & 1][k >> 1] = total[:, :middle]
        outs[2 + (k >> 1)][k & 1] = total[:, middle:]


def late_kernel(later, block, *refs):
    sums, outs = refs[:4], refs[4:]
    middle = block.shape[1] // 2
    for k in range(4):
        total = jnp.dot(later[k], block[...], preferred_element_type=jnp.float32)
        outs[k & 1][k >> 1] = sums[k & 1][k >> 1] + total[:, :middle]
        outs[2 + (k >> 1)][k & 1] = sums[2 + (k >> 1)][k & 1] + total[:, middle:]


def fold_kernel(kept_a, came_a, kept_b, came_b, next_a, next_b):
    next_a[...] = kept_a[0] + came_a[0]
    next_b[...] = kept_b[0] + came_b[0]


def rows_kernel(bias, target, *refs):
    shares, (keyval, outgoing) = refs[:-2], refs[-2:]
    begin = 0
    for kept, near, far in zip(shares[::3], shares[1::3], shares[2::3]):
        cols = slice(begin, begin + far.shape[1])
        summed = kept[0] + near[0] + far[...] + bias[:, cols]
        keyval[:, cols] = summed.astype(jnp.bfloat16)
        begin = cols.stop
    rows = keyval[...]
    slots, count = outgoing.shape[0], rows.shape[0]
    hits = lax.broadcasted_iota(jnp.int32, (slots, count), 0) == target[...]
    onehot = hits.astype(jnp.float32)
    used = jnp.sum(onehot, 1, keepdims=True)
    moved = jnp.dot(onehot.astype(jnp.bfloat16), rows, preferred_element_type=jnp.float32)
    empty = bias[...].astype(jnp.bfloat16).astype(jnp.float32)
    outgoing[...] = jnp.where(used > 0, moved, empty).astype(jnp.bfloat16)


def turn(values, cosine, sine):
    half = HD // 2
    turned = jnp.concatenate([values[:, half:], values[:, :half]], -1)
    return values * cosine + turned * sine


def rotate_kernel(queries, cosine, sine, out):
    for h in range(queries.shape[1] // HD):
        cols = slice(h * HD, (h + 1) * HD)
        values = queries[:, cols].astype(jnp.float32)
        out[:, cols] = turn(values, cosine[...], sine[...]).astype(jnp.bfloat16)


def attend_kernel(queries, keyval, cosine, sine, start, *rest, group):
    out = rest[-1]
    count = keyval.shape[0]
    token = lax.broadcasted_iota(jnp.int32, (count, count), 0)
    other = lax.broadcasted_iota(jnp.int32, (count, count), 1)
    allowed = (other >= start[...]) & (other <= token)
    mask = jnp.where(allowed, jnp.float32(0.0), jnp.float32(-1e30))
    half = count // 2
    keys = turn(keyval[:, :HD].astype(jnp.float32), cosine[...], sine[...])
    keys = keys.astype(jnp.bfloat16)
    values = keyval[:, HD:]
    for first, reach in ((0, half), (half, count)):
        rows = slice(first, first + half)
        stacked = jnp.concatenate(
            [queries[rows, h * HD : (h + 1) * HD] for h in range(group)], 0
        )
        scores = lax.dot_general(
            stacked,
            keys[:reach],
            (((1,), (1,)), ((), ())),
            preferred_element_type=jnp.float32,
        )
        masked = scores.reshape(group, half, reach) * HD ** (-0.5) + mask[rows, :reach]
        top = jnp.max(masked, -1, keepdims=True)
        weights = jnp.exp(masked - top)
        total = jnp.sum(weights, -1, keepdims=True)
        probs = (weights * (1.0 / total)).astype(jnp.bfloat16)
        mixed = jnp.dot(
            probs.reshape(group * half, reach),
            values[:reach],
            preferred_element_type=jnp.float32,
        ).astype(jnp.bfloat16)
        for h in range(group):
            out[rows, h * HD : (h + 1) * HD] = mixed[h * half : (h + 1) * half]


def chunks_of(heads):
    sizes = [heads // 2, heads - heads // 2]
    return [(sum(sizes[:i]), size) for i, size in enumerate(sizes) if size]


def shards(hidden, queries, lengths, scoring_rank, norm_gain, kv_weight, kv_bias):
    ranks = lax.axis_size("fz") * 2
    steps = ranks // 2
    count, features = hidden.shape
    width = features * lax.axis_size("tp")
    depth, columns = kv_weight.shape
    piece = depth // 2
    heads = columns // (2 * HD)
    group = queries.shape[1] // HD // heads
    capacity = 2 * count // ranks
    slots = capacity * ranks

    y = lax.axis_index("groups")
    core = lax.axis_index("tp")
    x, z = lax.axis_index("fx"), lax.axis_index("fz")
    place = jnp.stack([x, y, z, core]).astype(jnp.int32)

    right = [(i, (i + 1) % steps) for i in range(steps)]
    left = [(i, (i - 1) % steps) for i in range(steps)]
    flip = [(0, 1), (1, 0)]
    flip_both = [(i, 3 - i) for i in range(4)]

    def to_chip(k, array):
        if k == 1:
            return lax.ppermute(array, "fx", flip)
        if k == 2:
            return lax.ppermute(array, "groups", flip)
        return lax.ppermute(array, ("groups", "fx"), flip_both)

    hidden_f = hidden.astype(jnp.float32)
    ahead = lax.dynamic_slice(kv_weight, (y * piece, 0), (piece, chunks_of(heads)[0][1] * 2 * HD))
    squares = pl.pallas_call(
        squares_kernel,
        out_shape=jax.ShapeDtypeStruct((count, 1), jnp.float32),
        in_specs=[VMEM],
        out_specs=VMEM,
        compiler_params=PARAMS,
        cost_estimate=cost(2 * count * features, 1 << 20),
        name="squares",
    )(after(hidden, ahead))

    chunks = chunks_of(heads)
    gathered = []

    def gather(first, number, *waits):
        cut = (piece, number * 2 * HD)
        if not gathered:
            source, end = kv_weight, squares
        else:
            source, end = after(kv_weight, gathered[-1][-1], *waits), gathered[-1][steps // 2]
        block = lax.dynamic_slice(source, (y * piece, first * 2 * HD), cut) if gathered else ahead
        ups, downs = [block], [after(block, end)]
        for _ in range(steps // 2):
            ups.append(lax.ppermute(ups[-1], "fz", right))
        for _ in range((steps - 1) // 2):
            downs.append(lax.ppermute(downs[-1], "fz", left))
        gathered.append(ups + downs[:0:-1])

    for chunk in chunks:
        gather(*chunk)

    squares = squares + lax.ppermute(squares, "tp", flip)
    inverse_rms = lax.rsqrt(squares / width + EPSILON)
    slices = features // (4 * piece)
    if piece % HD == 0:
        normed = pl.pallas_call(
            functools.partial(norm_kernel, slices=slices, piece=piece),
            out_shape=[jax.ShapeDtypeStruct((count, features // 4), jnp.bfloat16)] * 4,
            in_specs=[SMEM] + [VMEM] * 3,
            out_specs=[VMEM] * 4,
            compiler_params=PARAMS,
            cost_estimate=cost(3 * count * features, 4 * count * features),
            name="norm",
        )(place, hidden, inverse_rms, norm_gain[None, :])
    else:
        whole = (hidden_f * inverse_rms * norm_gain[None, :]).astype(jnp.bfloat16)
        whole = whole.reshape(count, slices, 2, 2, piece)
        normed = []
        for k in range(4):
            part = lax.dynamic_index_in_dim(whole, x ^ (k & 1), 2, False)
            part = lax.dynamic_index_in_dim(part, y ^ (k >> 1), 2, False)
            normed.append(part.reshape(count, features // 4))
    own = [normed[0]] + [to_chip(k, normed[k]) for k in (1, 2, 3)]
    late = [after(own[0], own[2]), after(own[1], gathered[0][1])]
    peer = [lax.ppermute(block, "tp", flip) for block in late + own[2:]]

    dest = scoring_rank[:, 0]
    index = jnp.arange(count, dtype=jnp.int32)
    earlier = (dest[:, None] == dest[None, :]) & (index[:, None] < index[None, :])
    slot = jnp.sum(earlier.astype(jnp.int32), 0)
    target = dest * capacity + slot
    row = lengths[0]
    ends = jnp.cumsum(row)
    starts = ends - row
    within = (index[:, None] >= starts[None, :]) & (index[:, None] < ends[None, :])
    start = jnp.sum(jnp.where(within, starts[None, :], 0), 1)
    position = index - start
    freq = THETA ** (-jnp.arange(HD // 2, dtype=jnp.float32) * 2.0 / HD)
    angles = position.astype(jnp.float32)[:, None] * freq[None, :]
    cosine, sine = jnp.cos(angles), jnp.sin(angles)
    cosine = jnp.concatenate([cosine, cosine], 1)
    sine = jnp.concatenate([-sine, sine], 1)
    turned = pl.pallas_call(
        rotate_kernel,
        out_shape=jax.ShapeDtypeStruct(queries.shape, jnp.bfloat16),
        in_specs=[VMEM] * 3,
        out_specs=VMEM,
        compiler_params=PARAMS,
        cost_estimate=cost(4 * count * queries.shape[1], 4 * count * queries.shape[1]),
        name="rotate",
    )(queries, cosine, sine)

    bias = kv_bias[None, :]
    def begin_sums(blocks, sums, wide):
        order = [s for s in range(steps) if s != steps // 2]
        return pl.pallas_call(
            functools.partial(early_kernel, count=steps, piece=piece, order=order),
            out_shape=sums + [jax.ShapeDtypeStruct((4, count, piece), jnp.bfloat16)],
            in_specs=[SMEM] + [ANY] * (7 + steps),
            out_specs=[VMEM] * 5,
            scratch_shapes=[
                pltpu.VMEM((8, count, steps * piece // 2), jnp.bfloat16),
                pltpu.VMEM((steps - 1, piece, wide), jnp.bfloat16),
                pltpu.SemaphoreType.DMA((8,)),
                pltpu.SemaphoreType.DMA((steps - 1,)),
            ],
            compiler_params=FULL,
            cost_estimate=cost(2 * 3 * count * steps * piece * wide, 1 << 20),
            name="early",
        )(place, *own, *peer, *[blocks[s] for s in order])

    def all_of(*shape):
        return pl.BlockSpec(shape, lambda i: (0, 0))

    def add_up(n, begun, waits, meanwhile):
        wide = chunks[n][1] * 2 * HD
        middle = wide // 2
        sums = [jax.ShapeDtypeStruct((2, count, middle), jnp.float32)] * 4
        blocks = gathered[n]
        flops = 2 * 4 * count * steps * piece * wide
        if begun is None:
            parts = pl.pallas_call(
                functools.partial(matmul_kernel, count=steps, piece=piece),
                out_shape=sums,
                in_specs=[SMEM] + [ANY] * (8 + steps),
                out_specs=[VMEM] * 4,
                scratch_shapes=[
                    pltpu.VMEM((8, count, steps * piece // 2), jnp.bfloat16),
                    pltpu.VMEM((steps * piece, wide), jnp.bfloat16),
                    pltpu.SemaphoreType.DMA((8,)),
                    pltpu.SemaphoreType.DMA((steps,)),
                ],
                compiler_params=FULL,
                cost_estimate=cost(flops, 1 << 20),
                name="project",
            )(after(place, *waits), *own, *peer, *blocks)
        else:
            *parts, later = begun
            parts = pl.pallas_call(
                late_kernel,
                out_shape=[pltpu.HBM(sums[0].shape, jnp.float32), sums[1]] * 2,
                grid=(1,),
                in_specs=[VMEM] * 6,
                out_specs=[pl.BlockSpec((2, count, middle), lambda i: (0, 0, 0)), VMEM] * 2,
                compiler_params=PARAMS,
                cost_estimate=cost(flops // 4, 1 << 20),
                name="late",
            )(after(later, *waits), blocks[steps // 2], *parts)
        kept_a, sent_a, kept_b, sent_b = parts
        near_a, near_b = to_chip(1, sent_a), to_chip(2, sent_b)
        near_a = after(near_a, *meanwhile)
        second = pl.BlockSpec((1, count, middle), lambda i: (1, 0, 0))
        next_a, next_b = pl.pallas_call(
            fold_kernel,
            out_shape=[jax.ShapeDtypeStruct((count, middle), jnp.float32)] * 2,
            grid=(1,),
            in_specs=[second] * 4,
            out_specs=[all_of(count, middle)] * 2,
            compiler_params=PARAMS,
            cost_estimate=cost(2 * count * wide, 1 << 18),
            name="fold",
        )(kept_a, near_a, kept_b, near_b)
        return [kept_a, near_a, to_chip(2, next_a), kept_b, near_b, to_chip(1, next_b)]

    def rows_of(begin, shares, waits):
        wide = 2 * sum(share[2].shape[1] for share in shares)
        first_half = [
            pl.BlockSpec((1, count, share[2].shape[1]), lambda i: (0, 0, 0)) for share in shares
        ]
        specs = [
            [half, half, all_of(count, share[2].shape[1])] * 2
            for half, share in zip(first_half, shares)
        ]
        keyval, outgoing = pl.pallas_call(
            rows_kernel,
            out_shape=[
                pltpu.HBM((count, wide), jnp.bfloat16),
                pltpu.HBM((slots, wide), jnp.bfloat16),
            ],
            grid=(1,),
            in_specs=[all_of(1, wide), all_of(1, count)] + sum(specs, []),
            out_specs=[all_of(count, wide), all_of(slots, wide)],
            compiler_params=PARAMS,
            cost_estimate=cost(2 * slots * count * wide, 1 << 20),
            name="rows",
        )(after(kv_bias[None, begin : begin + wide], *waits), target[None, :], *sum(shares, []))
        return keyval, outgoing

    def send(begin, outgoing, stored):
        wide = outgoing.shape[1]
        received = lax.all_to_all(outgoing, ("fz", "fx"), split_axis=0, concat_axis=0, tiled=True)
        stored = pl.pallas_call(
            lambda *refs: refs[-1].__setitem__(Ellipsis, refs[0][...]),
            out_shape=jax.ShapeDtypeStruct((slots, columns), jnp.bfloat16),
            grid=(1,),
            in_specs=[all_of(slots, wide)] + [ANY] * len(stored),
            out_specs=pl.BlockSpec((slots, wide), lambda i: (0, begin // wide)),
            input_output_aliases={1: 0} if stored else {},
            compiler_params=PARAMS,
            cost_estimate=cost(1, 1 << 19),
            name="store",
        )(received, *stored)
        return stored

    def attend(begin, keyval, before):
        first, number = begin // (2 * HD), keyval.shape[1] // (2 * HD)
        return pl.pallas_call(
            functools.partial(attend_kernel, group=group),
            out_shape=jax.ShapeDtypeStruct(queries.shape, jnp.bfloat16),
            grid=(number,),
            in_specs=[
                pl.BlockSpec((count, group * HD), lambda i: (0, first + i)),
                pl.BlockSpec((count, 2 * HD), lambda i: (0, i)),
                all_of(count, HD),
                all_of(count, HD),
                all_of(count, 1),
            ]
            + [ANY] * len(before),
            out_specs=pl.BlockSpec((count, group * HD), lambda i: (0, first + i)),
            input_output_aliases={5: 0} if before else {},
            compiler_params=PARAMS,
            cost_estimate=cost(4 * number * group * count * count * HD, 1 << 20),
            name="attend",
        )(turned, keyval, cosine, sine, start[:, None], *before)

    begun = None
    if piece % HD == 0:
        wide = chunks[-1][1] * 2 * HD
        sums = [jax.ShapeDtypeStruct((2, count, wide // 2), jnp.float32)] * 4
        begun = begin_sums(gathered[-1], sums, wide)
    ready = [add_up(0, None, (turned, target, start), (gathered[1][1],))]
    for n in range(1, len(chunks) - 1):
        ready.append(add_up(n, None, (ready[-1][0],)))
    split = chunks[1][0] * 2 * HD
    keyval, outgoing = rows_of(0, ready[:1], (gathered[1][-1], *([] if begun is None else begun[:1])))
    attended = attend(0, keyval, [])
    ready.append(add_up(len(chunks) - 1, begun, (keyval,), (attended,)))
    stored = send(0, after(outgoing, ready[1][0]), [])
    keyval, outgoing = rows_of(split, ready[1:], (attended,))
    stored = send(split, outgoing, [stored])
    return (attend(split, keyval, [attended]), stored)


def solution(mesh):
    groups, ranks, cores = (mesh.shape[name] for name in ("groups", "fsdp", "tp"))
    devices = mesh.devices.reshape(groups, ranks // 2, 2, cores)
    paired = jax.sharding.Mesh(devices, ("groups", "fz", "fx", "tp"))
    rows = ("groups", "fz", "fx")
    placed = (
        P(rows, "tp"),
        P(rows, "tp"),
        P(rows, None),
        P(rows, None),
        P("tp"),
        P(("fz", "fx"), "tp"),
        P("tp"),
    )
    return jax.shard_map(
        shards,
        mesh=paired,
        in_specs=placed,
        out_specs=(P(rows, "tp"), P(rows, "tp")),
        check_vma=False,
    )
```

```python
import functools

import jax
import jax.numpy as jnp
from jax import lax
from jax.experimental import pallas as pl
from jax.experimental.pallas import tpu as pltpu
from jax.sharding import PartitionSpec as P

HD = 128
EPSILON = 1e-06
THETA = 1000000.0
VMEM = pl.BlockSpec(memory_space=pltpu.VMEM)
SMEM = pl.BlockSpec(memory_space=pltpu.SMEM)
FULL = pltpu.CompilerParams(vmem_limit_bytes=40 * 1024 * 1024)
ANY = pl.BlockSpec(memory_space=pl.ANY)
PARAMS = pltpu.CompilerParams(vmem_limit_bytes=16 * 1024 * 1024)


def after(value, *others):
    return lax.optimization_barrier((value, *others))[0]


def cost(flops, nbytes):
    return pl.CostEstimate(flops=flops, bytes_accessed=nbytes, transcendentals=0)


def squares_kernel(hidden, out):
    values = hidden[...].astype(jnp.float32)
    out[...] = jnp.sum(values * values, -1, keepdims=True)


def norm_kernel(place, hidden, inverse, gain, *outs, slices, piece):
    for k, out in enumerate(outs):
        x = place[0] ^ (k & 1)
        y = place[1] ^ (k >> 1)
        for i in range(slices):
            start = pl.multiple_of((i * 4 + x * 2 + y) * piece, piece)
            cols = pl.ds(start, piece)
            values = hidden[:, cols].astype(jnp.float32) * inverse[...] * gain[:, cols]
            out[:, i * piece : (i + 1) * piece] = values.astype(jnp.bfloat16)


def matmul_kernel(place, *refs, count, piece):
    rows = refs[:8]
    blocks = refs[8 : 8 + count]
    outs = refs[8 + count : -4]
    held, weights, row_sems, sems = refs[-4:]
    z, core = place[2], place[3]
    copies = []
    for s, block in enumerate(blocks):
        at = pl.multiple_of(lax.rem(z - s + count, count) * piece, piece)
        copies.append(pltpu.make_async_copy(block, weights.at[pl.ds(at, piece), :], sems.at[s]))
    loads = [pltpu.make_async_copy(rows[i], held.at[i], row_sems.at[i]) for i in range(8)]
    for copy in copies:
        copy.start()
    for k in range(4):
        loads[k].start()
        loads[4 + k].start()
    for copy in copies:
        copy.wait()
    half = count // 2 * piece
    mine = pl.ds(pl.multiple_of(core * half, half), half)
    others = pl.ds(pl.multiple_of((1 - core) * half, half), half)
    middle = weights.shape[1] // 2
    for k in range(4):
        loads[k].wait()
        loads[4 + k].wait()
        total = jnp.dot(
            held[k], weights[mine, :], preferred_element_type=jnp.float32
        ) + jnp.dot(held[4 + k], weights[others, :], preferred_element_type=jnp.float32)
        outs[k & 1][k >> 1] = total[:, :middle]
        outs[2 + (k >> 1)][k & 1] = total[:, middle:]


def early_kernel(place, *refs, count, piece, order):
    rows, blocks, outs, later = refs[:8], refs[8:-9], refs[-9:-5], refs[-5]
    held, weights, row_sems, sems = refs[-4:]
    z, core = place[2], place[3]
    copies = [
        pltpu.make_async_copy(block, weights.at[i], sems.at[i]) for i, block in enumerate(blocks)
    ]
    loads = [pltpu.make_async_copy(rows[i], held.at[i], row_sems.at[i]) for i in range(8)]
    for copy in copies:
        copy.start()
    for k in range(4):
        loads[k].start()
        loads[4 + k].start()
    for copy in copies:
        copy.wait()
    half = count // 2
    middle = weights.shape[2] // 2

    def features(k, s):
        at = lax.rem(z - s + count, count)
        side = jnp.where(lax.div(at, half) == core, 0, 4)
        cols = pl.ds(pl.multiple_of(lax.rem(at, half) * piece, piece), piece)
        return held[side + k, :, cols]

    for k in range(4):
        loads[k].wait()
        loads[4 + k].wait()
        later[k] = features(k, count // 2)
        total = None
        for i, s in enumerate(order):
            part = jnp.dot(features(k, s), weights[i], preferred_element_type=jnp.float32)
            total = part if total is None else total + part
        outs[k & 1][k >> 1] = total[:, :middle]
        outs[2 + (k >> 1)][k & 1] = total[:, middle:]


def late_kernel(later, block, *refs):
    sums, outs = refs[:4], refs[4:]
    middle = block.shape[1] // 2
    for k in range(4):
        total = jnp.dot(later[k], block[...], preferred_element_type=jnp.float32)
        outs[k & 1][k >> 1] = sums[k & 1][k >> 1] + total[:, :middle]
        outs[2 + (k >> 1)][k & 1] = sums[2 + (k >> 1)][k & 1] + total[:, middle:]


def fold_kernel(kept_a, came_a, kept_b, came_b, next_a, next_b):
    next_a[...] = kept_a[0] + came_a[0]
    next_b[...] = kept_b[0] + came_b[0]


def rows_kernel(bias, target, *refs):
    shares, (keyval, outgoing) = refs[:-2], refs[-2:]
    begin = 0
    for kept, near, far in zip(shares[::3], shares[1::3], shares[2::3]):
        cols = slice(begin, begin + far.shape[1])
        summed = kept[0] + near[0] + far[...] + bias[:, cols]
        keyval[:, cols] = summed.astype(jnp.bfloat16)
        begin = cols.stop
    rows = keyval[...]
    slots, count = outgoing.shape[0], rows.shape[0]
    hits = lax.broadcasted_iota(jnp.int32, (slots, count), 0) == target[...]
    onehot = hits.astype(jnp.float32)
    used = jnp.sum(onehot, 1, keepdims=True)
    moved = jnp.dot(onehot.astype(jnp.bfloat16), rows, preferred_element_type=jnp.float32)
    empty = bias[...].astype(jnp.bfloat16).astype(jnp.float32)
    outgoing[...] = jnp.where(used > 0, moved, empty).astype(jnp.bfloat16)


def turn(values, cosine, sine):
    half = HD // 2
    turned = jnp.concatenate([values[:, half:], values[:, :half]], -1)
    return values * cosine + turned * sine


def rotate_kernel(queries, cosine, sine, out):
    for h in range(queries.shape[1] // HD):
        cols = slice(h * HD, (h + 1) * HD)
        values = queries[:, cols].astype(jnp.float32)
        out[:, cols] = turn(values, cosine[...], sine[...]).astype(jnp.bfloat16)


def attend_kernel(queries, keyval, cosine, sine, start, *rest, group):
    out = rest[-1]
    count = keyval.shape[0]
    token = lax.broadcasted_iota(jnp.int32, (count, count), 0)
    other = lax.broadcasted_iota(jnp.int32, (count, count), 1)
    allowed = (other >= start[...]) & (other <= token)
    mask = jnp.where(allowed, jnp.float32(0.0), jnp.float32(-1e30))
    half = count // 2
    keys = turn(keyval[:, :HD].astype(jnp.float32), cosine[...], sine[...])
    keys = keys.astype(jnp.bfloat16)
    values = keyval[:, HD:]
    for first, reach in ((0, half), (half, count)):
        rows = slice(first, first + half)
        stacked = jnp.concatenate(
            [queries[rows, h * HD : (h + 1) * HD] for h in range(group)], 0
        )
        scores = lax.dot_general(
            stacked,
            keys[:reach],
            (((1,), (1,)), ((), ())),
            preferred_element_type=jnp.float32,
        )
        masked = scores.reshape(group, half, reach) * HD ** (-0.5) + mask[rows, :reach]
        top = jnp.max(masked, -1, keepdims=True)
        weights = jnp.exp(masked - top)
        total = jnp.sum(weights, -1, keepdims=True)
        probs = (weights * (1.0 / total)).astype(jnp.bfloat16)
        mixed = jnp.dot(
            probs.reshape(group * half, reach),
            values[:reach],
            preferred_element_type=jnp.float32,
        ).astype(jnp.bfloat16)
        for h in range(group):
            out[rows, h * HD : (h + 1) * HD] = mixed[h * half : (h + 1) * half]


def chunks_of(heads):
    sizes = [heads // 2] + [1] * (heads - heads // 2)
    return [(sum(sizes[:i]), size) for i, size in enumerate(sizes) if size]


def shards(hidden, queries, lengths, scoring_rank, norm_gain, kv_weight, kv_bias):
    ranks = lax.axis_size("fz") * 2
    steps = ranks // 2
    count, features = hidden.shape
    width = features * lax.axis_size("tp")
    depth, columns = kv_weight.shape
    piece = depth // 2
    heads = columns // (2 * HD)
    group = queries.shape[1] // HD // heads
    capacity = 2 * count // ranks
    slots = capacity * ranks

    y = lax.axis_index("groups")
    core = lax.axis_index("tp")
    x, z = lax.axis_index("fx"), lax.axis_index("fz")
    place = jnp.stack([x, y, z, core]).astype(jnp.int32)

    right = [(i, (i + 1) % steps) for i in range(steps)]
    left = [(i, (i - 1) % steps) for i in range(steps)]
    flip = [(0, 1), (1, 0)]
    flip_both = [(i, 3 - i) for i in range(4)]

    def to_chip(k, array):
        if k == 1:
            return lax.ppermute(array, "fx", flip)
        if k == 2:
            return lax.ppermute(array, "groups", flip)
        return lax.ppermute(array, ("groups", "fx"), flip_both)

    hidden_f = hidden.astype(jnp.float32)
    ahead = lax.dynamic_slice(kv_weight, (y * piece, 0), (piece, chunks_of(heads)[0][1] * 2 * HD))
    squares = pl.pallas_call(
        squares_kernel,
        out_shape=jax.ShapeDtypeStruct((count, 1), jnp.float32),
        in_specs=[VMEM],
        out_specs=VMEM,
        compiler_params=PARAMS,
        cost_estimate=cost(2 * count * features, 1 << 20),
        name="squares",
    )(after(hidden, ahead))

    chunks = chunks_of(heads)
    gathered = []

    def gather(first, number, relay=()):
        cut = (piece, number * 2 * HD)
        if not gathered:
            source, end = kv_weight, squares
        else:
            source, end = after(kv_weight, gathered[-1][-1]), gathered[-1][steps // 2]
        block = lax.dynamic_slice(source, (y * piece, first * 2 * HD), cut) if gathered else ahead
        ups, downs = [block], [after(block, end)]
        for i in range(steps // 2):
            held = after(ups[-1], *relay) if relay and i == 1 else ups[-1]
            ups.append(lax.ppermute(held, "fz", right))
        for _ in range((steps - 1) // 2):
            downs.append(lax.ppermute(downs[-1], "fz", left))
        gathered.append(ups + downs[:0:-1])

    gather(*chunks[0])

    squares = squares + lax.ppermute(squares, "tp", flip)
    inverse_rms = lax.rsqrt(squares / width + EPSILON)
    slices = features // (4 * piece)
    if piece % HD == 0:
        normed = pl.pallas_call(
            functools.partial(norm_kernel, slices=slices, piece=piece),
            out_shape=[jax.ShapeDtypeStruct((count, features // 4), jnp.bfloat16)] * 4,
            in_specs=[SMEM] + [VMEM] * 3,
            out_specs=[VMEM] * 4,
            compiler_params=PARAMS,
            cost_estimate=cost(3 * count * features, 4 * count * features),
            name="norm",
        )(place, hidden, inverse_rms, norm_gain[None, :])
    else:
        whole = (hidden_f * inverse_rms * norm_gain[None, :]).astype(jnp.bfloat16)
        whole = whole.reshape(count, slices, 2, 2, piece)
        normed = []
        for k in range(4):
            part = lax.dynamic_index_in_dim(whole, x ^ (k & 1), 2, False)
            part = lax.dynamic_index_in_dim(part, y ^ (k >> 1), 2, False)
            normed.append(part.reshape(count, features // 4))
    own = [normed[0]] + [to_chip(k, normed[k]) for k in (1, 2, 3)]
    late = [after(own[0], own[2]), after(own[1], gathered[0][1])]
    peer = [lax.ppermute(block, "tp", flip) for block in late + own[2:]]

    dest = scoring_rank[:, 0]
    index = jnp.arange(count, dtype=jnp.int32)
    earlier = (dest[:, None] == dest[None, :]) & (index[:, None] < index[None, :])
    slot = jnp.sum(earlier.astype(jnp.int32), 0)
    target = dest * capacity + slot
    row = lengths[0]
    ends = jnp.cumsum(row)
    starts = ends - row
    within = (index[:, None] >= starts[None, :]) & (index[:, None] < ends[None, :])
    start = jnp.sum(jnp.where(within, starts[None, :], 0), 1)
    position = index - start
    freq = THETA ** (-jnp.arange(HD // 2, dtype=jnp.float32) * 2.0 / HD)
    angles = position.astype(jnp.float32)[:, None] * freq[None, :]
    cosine, sine = jnp.cos(angles), jnp.sin(angles)
    cosine = jnp.concatenate([cosine, cosine], 1)
    sine = jnp.concatenate([-sine, sine], 1)
    turned = pl.pallas_call(
        rotate_kernel,
        out_shape=jax.ShapeDtypeStruct(queries.shape, jnp.bfloat16),
        in_specs=[VMEM] * 3,
        out_specs=VMEM,
        compiler_params=PARAMS,
        cost_estimate=cost(4 * count * queries.shape[1], 4 * count * queries.shape[1]),
        name="rotate",
    )(queries, cosine, sine)

    bias = kv_bias[None, :]
    def begin_sums(blocks, sums, wide):
        order = [s for s in range(steps) if s != steps // 2]
        return pl.pallas_call(
            functools.partial(early_kernel, count=steps, piece=piece, order=order),
            out_shape=sums + [jax.ShapeDtypeStruct((4, count, piece), jnp.bfloat16)],
            in_specs=[SMEM] + [ANY] * (7 + steps),
            out_specs=[VMEM] * 5,
            scratch_shapes=[
                pltpu.VMEM((8, count, steps * piece // 2), jnp.bfloat16),
                pltpu.VMEM((steps - 1, piece, wide), jnp.bfloat16),
                pltpu.SemaphoreType.DMA((8,)),
                pltpu.SemaphoreType.DMA((steps - 1,)),
            ],
            compiler_params=FULL,
            cost_estimate=cost(2 * 3 * count * steps * piece * wide, 1 << 20),
            name="early",
        )(place, *own, *peer, *[blocks[s] for s in order])

    def all_of(*shape):
        return pl.BlockSpec(shape, lambda i: (0, 0))

    def add_up(n, begun, waits):
        wide = chunks[n][1] * 2 * HD
        middle = wide // 2
        sums = [jax.ShapeDtypeStruct((2, count, middle), jnp.float32)] * 4
        blocks = gathered[n]
        flops = 2 * 4 * count * steps * piece * wide
        if begun is None:
            parts = pl.pallas_call(
                functools.partial(matmul_kernel, count=steps, piece=piece),
                out_shape=[pltpu.HBM(each.shape, each.dtype) for each in sums] if n else sums,
                grid=(1,),
                in_specs=[SMEM] + [ANY] * (8 + steps),
                out_specs=[pl.BlockSpec((2, count, middle), lambda i: (0, 0, 0)) if n else VMEM] * 4,
                scratch_shapes=[
                    pltpu.VMEM((8, count, steps * piece // 2), jnp.bfloat16),
                    pltpu.VMEM((steps * piece, wide), jnp.bfloat16),
                    pltpu.SemaphoreType.DMA((8,)),
                    pltpu.SemaphoreType.DMA((steps,)),
                ],
                compiler_params=FULL,
                cost_estimate=cost(flops, 1 << 20),
                name="project",
            )(after(place, *waits), *own, *peer, *blocks)
        else:
            *parts, later = begun
            parts = pl.pallas_call(
                late_kernel,
                out_shape=[pltpu.HBM(each.shape, each.dtype) for each in sums],
                grid=(1,),
                in_specs=[VMEM] * 6,
                out_specs=[pl.BlockSpec((2, count, middle), lambda i: (0, 0, 0))] * 4,
                compiler_params=PARAMS,
                cost_estimate=cost(flops // 4, 1 << 20),
                name="late",
            )(after(later, *waits), blocks[steps // 2], *parts)
        return parts

    def exchange(n, parts, waits):
        middle = chunks[n][1] * HD
        wide = 2 * middle
        kept_a, sent_a, kept_b, sent_b = parts
        near_a, near_b = to_chip(1, sent_a), to_chip(2, sent_b)
        near_a = after(near_a, *waits)
        second = pl.BlockSpec((1, count, middle), lambda i: (1, 0, 0))
        next_a, next_b = pl.pallas_call(
            fold_kernel,
            out_shape=[jax.ShapeDtypeStruct((count, middle), jnp.float32)] * 2,
            grid=(1,),
            in_specs=[second] * 4,
            out_specs=[all_of(count, middle)] * 2,
            compiler_params=PARAMS,
            cost_estimate=cost(2 * count * wide, 1 << 18),
            name="fold",
        )(kept_a, near_a, kept_b, near_b)
        return next_a, [kept_a, near_a, to_chip(2, next_a), kept_b, near_b, to_chip(1, next_b)]

    def rows_of(begin, shares, waits):
        wide = 2 * sum(share[2].shape[1] for share in shares)
        first_half = [
            pl.BlockSpec((1, count, share[2].shape[1]), lambda i: (0, 0, 0)) for share in shares
        ]
        specs = [
            [half, half, all_of(count, share[2].shape[1])] * 2
            for half, share in zip(first_half, shares)
        ]
        keyval, outgoing = pl.pallas_call(
            rows_kernel,
            out_shape=[
                pltpu.HBM((count, wide), jnp.bfloat16),
                pltpu.HBM((slots, wide), jnp.bfloat16),
            ],
            grid=(1,),
            in_specs=[all_of(1, wide), all_of(1, count)] + sum(specs, []),
            out_specs=[all_of(count, wide), all_of(slots, wide)],
            compiler_params=PARAMS,
            cost_estimate=cost(2 * slots * count * wide, 1 << 20),
            name="rows",
        )(after(kv_bias[None, begin : begin + wide], *waits), target[None, :], *sum(shares, []))
        return keyval, outgoing

    def send(begin, outgoing, stored):
        wide = outgoing.shape[1]
        received = lax.all_to_all(outgoing, ("fz", "fx"), split_axis=0, concat_axis=0, tiled=True)
        stored = pl.pallas_call(
            lambda *refs: refs[-1].__setitem__(Ellipsis, refs[0][...]),
            out_shape=jax.ShapeDtypeStruct((slots, columns), jnp.bfloat16),
            grid=(1,),
            in_specs=[all_of(slots, wide)] + [ANY] * len(stored),
            out_specs=pl.BlockSpec((slots, wide), lambda i: (0, begin // wide)),
            input_output_aliases={1: 0} if stored else {},
            compiler_params=PARAMS,
            cost_estimate=cost(1, 1 << 19),
            name="store",
        )(received, *stored)
        return stored

    def attend(begin, keyval, before):
        first, number = begin // (2 * HD), keyval.shape[1] // (2 * HD)
        return pl.pallas_call(
            functools.partial(attend_kernel, group=group),
            out_shape=jax.ShapeDtypeStruct(queries.shape, jnp.bfloat16),
            grid=(number,),
            in_specs=[
                pl.BlockSpec((count, group * HD), lambda i: (0, first + i)),
                pl.BlockSpec((count, 2 * HD), lambda i: (0, i)),
                all_of(count, HD),
                all_of(count, HD),
                all_of(count, 1),
            ]
            + [ANY] * len(before),
            out_specs=pl.BlockSpec((count, group * HD), lambda i: (0, first + i)),
            input_output_aliases={5: 0} if before else {},
            compiler_params=PARAMS,
            cost_estimate=cost(4 * number * group * count * count * HD, 1 << 20),
            name="attend",
        )(turned, keyval, cosine, sine, start[:, None], *before)

    parts_0 = add_up(0, None, (turned, target, start))
    gather(*chunks[1], relay=(parts_0[0],))
    gather(*chunks[2])
    begun = None
    if piece % HD == 0:
        wide = chunks[-1][1] * 2 * HD
        sums = [jax.ShapeDtypeStruct((2, count, wide // 2), jnp.float32)] * 4
        begun = begin_sums(gathered[-1], sums, wide)
    parts_1 = add_up(1, None, (parts_0[0],))
    _, share_0 = exchange(0, parts_0, (parts_1[0], gathered[1][-1]))
    folded, share_1 = exchange(1, parts_1, (gathered[2][-1], *([] if begun is None else begun[:1])))
    split = chunks[1][0] * 2 * HD
    keyval, outgoing = rows_of(0, [share_0], (*([] if begun is None else begun[:1]),))
    attended = attend(0, keyval, [])
    parts_2 = add_up(2, begun, (keyval, folded))
    _, share_2 = exchange(2, parts_2, (attended,))
    stored = send(0, after(outgoing, parts_2[0]), [])
    keyval, outgoing = rows_of(split, [share_1, share_2], (attended,))
    stored = send(split, outgoing, [stored])
    return (attend(split, keyval, [attended]), stored)


def solution(mesh):
    groups, ranks, cores = (mesh.shape[name] for name in ("groups", "fsdp", "tp"))
    devices = mesh.devices.reshape(groups, ranks // 2, 2, cores)
    paired = jax.sharding.Mesh(devices, ("groups", "fz", "fx", "tp"))
    rows = ("groups", "fz", "fx")
    placed = (
        P(rows, "tp"),
        P(rows, "tp"),
        P(rows, None),
        P(rows, None),
        P("tp"),
        P(("fz", "fx"), "tp"),
        P("tp"),
    )
    return jax.shard_map(
        shards,
        mesh=paired,
        in_specs=placed,
        out_specs=(P(rows, "tp"), P(rows, "tp")),
        check_vma=False,
    )
```

```python
import functools

import jax
import jax.numpy as jnp
from jax import lax
from jax.experimental import pallas as pl
from jax.experimental.pallas import tpu as pltpu
from jax.sharding import PartitionSpec as P

HD = 128
EPSILON = 1e-06
THETA = 1000000.0
VMEM = pl.BlockSpec(memory_space=pltpu.VMEM)
SMEM = pl.BlockSpec(memory_space=pltpu.SMEM)
FULL = pltpu.CompilerParams(vmem_limit_bytes=40 * 1024 * 1024)
ANY = pl.BlockSpec(memory_space=pl.ANY)
PARAMS = pltpu.CompilerParams(vmem_limit_bytes=16 * 1024 * 1024)


def after(value, *others):
    return lax.optimization_barrier((value, *others))[0]


def cost(flops, nbytes):
    return pl.CostEstimate(flops=flops, bytes_accessed=nbytes, transcendentals=0)


def squares_kernel(hidden, out):
    values = hidden[...].astype(jnp.float32)
    out[...] = jnp.sum(values * values, -1, keepdims=True)


def norm_kernel(place, hidden, inverse, gain, *outs, slices, piece):
    for k, out in enumerate(outs):
        x = place[0] ^ (k & 1)
        y = place[1] ^ (k >> 1)
        for i in range(slices):
            start = pl.multiple_of((i * 4 + x * 2 + y) * piece, piece)
            cols = pl.ds(start, piece)
            values = hidden[:, cols].astype(jnp.float32) * inverse[...] * gain[:, cols]
            out[:, i * piece : (i + 1) * piece] = values.astype(jnp.bfloat16)


def matmul_kernel(place, *refs, count, piece):
    rows = refs[:8]
    blocks = refs[8 : 8 + count]
    outs = refs[8 + count : -4]
    held, weights, row_sems, sems = refs[-4:]
    z, core = place[2], place[3]
    copies = []
    for s, block in enumerate(blocks):
        at = pl.multiple_of(lax.rem(z - s + count, count) * piece, piece)
        copies.append(pltpu.make_async_copy(block, weights.at[pl.ds(at, piece), :], sems.at[s]))
    loads = [pltpu.make_async_copy(rows[i], held.at[i], row_sems.at[i]) for i in range(8)]
    for copy in copies:
        copy.start()
    for k in range(4):
        loads[k].start()
        loads[4 + k].start()
    for copy in copies:
        copy.wait()
    half = count // 2 * piece
    mine = pl.ds(pl.multiple_of(core * half, half), half)
    others = pl.ds(pl.multiple_of((1 - core) * half, half), half)
    middle = weights.shape[1] // 2
    for k in range(4):
        loads[k].wait()
        loads[4 + k].wait()
        total = jnp.dot(
            held[k], weights[mine, :], preferred_element_type=jnp.float32
        ) + jnp.dot(held[4 + k], weights[others, :], preferred_element_type=jnp.float32)
        outs[k & 1][k >> 1] = total[:, :middle]
        outs[2 + (k >> 1)][k & 1] = total[:, middle:]


def early_kernel(place, *refs, count, piece, order):
    rows, blocks, outs, later = refs[:8], refs[8:-9], refs[-9:-5], refs[-5]
    held, weights, row_sems, sems = refs[-4:]
    z, core = place[2], place[3]
    copies = [
        pltpu.make_async_copy(block, weights.at[i], sems.at[i]) for i, block in enumerate(blocks)
    ]
    loads = [pltpu.make_async_copy(rows[i], held.at[i], row_sems.at[i]) for i in range(8)]
    for copy in copies:
        copy.start()
    for k in range(4):
        loads[k].start()
        loads[4 + k].start()
    for copy in copies:
        copy.wait()
    half = count // 2
    middle = weights.shape[2] // 2

    def features(k, s):
        at = lax.rem(z - s + count, count)
        side = jnp.where(lax.div(at, half) == core, 0, 4)
        cols = pl.ds(pl.multiple_of(lax.rem(at, half) * piece, piece), piece)
        return held[side + k, :, cols]

    for k in range(4):
        loads[k].wait()
        loads[4 + k].wait()
        later[k] = features(k, count // 2)
        total = None
        for i, s in enumerate(order):
            part = jnp.dot(features(k, s), weights[i], preferred_element_type=jnp.float32)
            total = part if total is None else total + part
        outs[k & 1][k >> 1] = total[:, :middle]
        outs[2 + (k >> 1)][k & 1] = total[:, middle:]


def late_kernel(later, block, *refs):
    sums, outs = refs[:4], refs[4:]
    middle = block.shape[1] // 2
    for k in range(4):
        total = jnp.dot(later[k], block[...], preferred_element_type=jnp.float32)
        outs[k & 1][k >> 1] = sums[k & 1][k >> 1] + total[:, :middle]
        outs[2 + (k >> 1)][k & 1] = sums[2 + (k >> 1)][k & 1] + total[:, middle:]


def fold_kernel(kept_a, came_a, kept_b, came_b, next_a, next_b):
    next_a[...] = kept_a[0] + came_a[0]
    next_b[...] = kept_b[0] + came_b[0]


def rows_kernel(bias, target, *refs):
    shares, (keyval, outgoing) = refs[:-2], refs[-2:]
    begin = 0
    for kept, near, far in zip(shares[::3], shares[1::3], shares[2::3]):
        cols = slice(begin, begin + far.shape[1])
        summed = kept[0] + near[0] + far[...] + bias[:, cols]
        keyval[:, cols] = summed.astype(jnp.bfloat16)
        begin = cols.stop
    rows = keyval[...]
    slots, count = outgoing.shape[0], rows.shape[0]
    hits = lax.broadcasted_iota(jnp.int32, (slots, count), 0) == target[...]
    onehot = hits.astype(jnp.float32)
    used = jnp.sum(onehot, 1, keepdims=True)
    moved = jnp.dot(onehot.astype(jnp.bfloat16), rows, preferred_element_type=jnp.float32)
    empty = bias[...].astype(jnp.bfloat16).astype(jnp.float32)
    outgoing[...] = jnp.where(used > 0, moved, empty).astype(jnp.bfloat16)


def turn(values, cosine, sine):
    half = HD // 2
    turned = jnp.concatenate([values[:, half:], values[:, :half]], -1)
    return values * cosine + turned * sine


def rotate_kernel(queries, cosine, sine, out):
    for h in range(queries.shape[1] // HD):
        cols = slice(h * HD, (h + 1) * HD)
        values = queries[:, cols].astype(jnp.float32)
        out[:, cols] = turn(values, cosine[...], sine[...]).astype(jnp.bfloat16)


def attend_kernel(queries, keyval, cosine, sine, start, *rest, group):
    out = rest[-1]
    count = keyval.shape[0]
    token = lax.broadcasted_iota(jnp.int32, (count, count), 0)
    other = lax.broadcasted_iota(jnp.int32, (count, count), 1)
    allowed = (other >= start[...]) & (other <= token)
    mask = jnp.where(allowed, jnp.float32(0.0), jnp.float32(-1e30))
    half = count // 2
    keys = turn(keyval[:, :HD].astype(jnp.float32), cosine[...], sine[...])
    keys = keys.astype(jnp.bfloat16)
    values = keyval[:, HD:]
    for first, reach in ((0, half), (half, count)):
        rows = slice(first, first + half)
        stacked = jnp.concatenate(
            [queries[rows, h * HD : (h + 1) * HD] for h in range(group)], 0
        )
        scores = lax.dot_general(
            stacked,
            keys[:reach],
            (((1,), (1,)), ((), ())),
            preferred_element_type=jnp.float32,
        )
        masked = scores.reshape(group, half, reach) * HD ** (-0.5) + mask[rows, :reach]
        top = jnp.max(masked, -1, keepdims=True)
        weights = jnp.exp(masked - top)
        total = jnp.sum(weights, -1, keepdims=True)
        probs = (weights * (1.0 / total)).astype(jnp.bfloat16)
        mixed = jnp.dot(
            probs.reshape(group * half, reach),
            values[:reach],
            preferred_element_type=jnp.float32,
        ).astype(jnp.bfloat16)
        for h in range(group):
            out[rows, h * HD : (h + 1) * HD] = mixed[h * half : (h + 1) * half]


def chunks_of(heads):
    sizes = [heads // 2] + [1] * (heads - heads // 2)
    return [(sum(sizes[:i]), size) for i, size in enumerate(sizes) if size]


def shards(hidden, queries, lengths, scoring_rank, norm_gain, kv_weight, kv_bias):
    ranks = lax.axis_size("fz") * 2
    steps = ranks // 2
    count, features = hidden.shape
    width = features * lax.axis_size("tp")
    depth, columns = kv_weight.shape
    piece = depth // 2
    heads = columns // (2 * HD)
    group = queries.shape[1] // HD // heads
    capacity = 2 * count // ranks
    slots = capacity * ranks

    y = lax.axis_index("groups")
    core = lax.axis_index("tp")
    x, z = lax.axis_index("fx"), lax.axis_index("fz")
    place = jnp.stack([x, y, z, core]).astype(jnp.int32)

    right = [(i, (i + 1) % steps) for i in range(steps)]
    left = [(i, (i - 1) % steps) for i in range(steps)]
    flip = [(0, 1), (1, 0)]
    flip_both = [(i, 3 - i) for i in range(4)]

    def to_chip(k, array):
        if k == 1:
            return lax.ppermute(array, "fx", flip)
        if k == 2:
            return lax.ppermute(array, "groups", flip)
        return lax.ppermute(array, ("groups", "fx"), flip_both)

    hidden_f = hidden.astype(jnp.float32)
    ahead = lax.dynamic_slice(kv_weight, (y * piece, 0), (piece, chunks_of(heads)[0][1] * 2 * HD))
    squares = pl.pallas_call(
        squares_kernel,
        out_shape=jax.ShapeDtypeStruct((count, 1), jnp.float32),
        in_specs=[VMEM],
        out_specs=VMEM,
        compiler_params=PARAMS,
        cost_estimate=cost(2 * count * features, 1 << 20),
        name="squares",
    )(after(hidden, ahead))

    chunks = chunks_of(heads)
    gathered = []

    def gather(first, number, relay=()):
        cut = (piece, number * 2 * HD)
        if not gathered:
            source, end = kv_weight, squares
        else:
            source, end = after(kv_weight, gathered[-1][-1]), gathered[-1][steps // 2]
        block = lax.dynamic_slice(source, (y * piece, first * 2 * HD), cut) if gathered else ahead
        ups, downs = [block], [after(block, end)]
        for i in range(steps // 2):
            held = after(ups[-1], *relay) if relay and i == 1 else ups[-1]
            ups.append(lax.ppermute(held, "fz", right))
        for _ in range((steps - 1) // 2):
            downs.append(lax.ppermute(downs[-1], "fz", left))
        gathered.append(ups + downs[:0:-1])

    gather(*chunks[0])

    squares = squares + lax.ppermute(squares, "tp", flip)
    inverse_rms = lax.rsqrt(squares / width + EPSILON)
    slices = features // (4 * piece)
    if piece % HD == 0:
        normed = pl.pallas_call(
            functools.partial(norm_kernel, slices=slices, piece=piece),
            out_shape=[jax.ShapeDtypeStruct((count, features // 4), jnp.bfloat16)] * 4,
            in_specs=[SMEM] + [VMEM] * 3,
            out_specs=[VMEM] * 4,
            compiler_params=PARAMS,
            cost_estimate=cost(3 * count * features, 4 * count * features),
            name="norm",
        )(place, hidden, inverse_rms, norm_gain[None, :])
    else:
        whole = (hidden_f * inverse_rms * norm_gain[None, :]).astype(jnp.bfloat16)
        whole = whole.reshape(count, slices, 2, 2, piece)
        normed = []
        for k in range(4):
            part = lax.dynamic_index_in_dim(whole, x ^ (k & 1), 2, False)
            part = lax.dynamic_index_in_dim(part, y ^ (k >> 1), 2, False)
            normed.append(part.reshape(count, features // 4))
    own = [normed[0]] + [to_chip(k, normed[k]) for k in (1, 2, 3)]
    index = jnp.arange(count, dtype=jnp.int32)
    row = lengths[0]
    ends = jnp.cumsum(row)
    starts = ends - row
    within = (index[:, None] >= starts[None, :]) & (index[:, None] < ends[None, :])
    start = jnp.sum(jnp.where(within, starts[None, :], 0), 1)
    position = index - start
    freq = THETA ** (-jnp.arange(HD // 2, dtype=jnp.float32) * 2.0 / HD)
    angles = position.astype(jnp.float32)[:, None] * freq[None, :]
    cosine, sine = jnp.cos(angles), jnp.sin(angles)
    cosine = jnp.concatenate([cosine, cosine], 1)
    sine = jnp.concatenate([-sine, sine], 1)
    turned = pl.pallas_call(
        rotate_kernel,
        out_shape=pltpu.HBM(queries.shape, jnp.bfloat16),
        grid=(1,),
        in_specs=[pl.BlockSpec(queries.shape, lambda i: (0, 0))]
        + [pl.BlockSpec((count, HD), lambda i: (0, 0))] * 2,
        out_specs=pl.BlockSpec(queries.shape, lambda i: (0, 0)),
        compiler_params=PARAMS,
        cost_estimate=cost(4 * count * queries.shape[1], 4 * count * queries.shape[1]),
        name="rotate",
    )(queries, cosine, sine)
    late = [after(own[0], own[2], turned), after(own[1], gathered[0][1])]
    peer = [lax.ppermute(block, "tp", flip) for block in late + own[2:]]

    dest = scoring_rank[:, 0]
    index = jnp.arange(count, dtype=jnp.int32)
    earlier = (dest[:, None] == dest[None, :]) & (index[:, None] < index[None, :])
    slot = jnp.sum(earlier.astype(jnp.int32), 0)
    target = dest * capacity + slot

    bias = kv_bias[None, :]
    def begin_sums(blocks, sums, wide):
        order = [s for s in range(steps) if s != steps // 2]
        return pl.pallas_call(
            functools.partial(early_kernel, count=steps, piece=piece, order=order),
            out_shape=sums + [jax.ShapeDtypeStruct((4, count, piece), jnp.bfloat16)],
            in_specs=[SMEM] + [ANY] * (7 + steps),
            out_specs=[VMEM] * 5,
            scratch_shapes=[
                pltpu.VMEM((8, count, steps * piece // 2), jnp.bfloat16),
                pltpu.VMEM((steps - 1, piece, wide), jnp.bfloat16),
                pltpu.SemaphoreType.DMA((8,)),
                pltpu.SemaphoreType.DMA((steps - 1,)),
            ],
            compiler_params=FULL,
            cost_estimate=cost(2 * 3 * count * steps * piece * wide, 1 << 20),
            name="early",
        )(place, *own, *peer, *[blocks[s] for s in order])

    def all_of(*shape):
        return pl.BlockSpec(shape, lambda i: (0, 0))

    def add_up(n, begun, waits):
        wide = chunks[n][1] * 2 * HD
        middle = wide // 2
        sums = [jax.ShapeDtypeStruct((2, count, middle), jnp.float32)] * 4
        blocks = gathered[n]
        flops = 2 * 4 * count * steps * piece * wide
        if begun is None:
            parts = pl.pallas_call(
                functools.partial(matmul_kernel, count=steps, piece=piece),
                out_shape=[pltpu.HBM(each.shape, each.dtype) for each in sums] if n else sums,
                grid=(1,),
                in_specs=[SMEM] + [ANY] * (8 + steps),
                out_specs=[pl.BlockSpec((2, count, middle), lambda i: (0, 0, 0)) if n else VMEM] * 4,
                scratch_shapes=[
                    pltpu.VMEM((8, count, steps * piece // 2), jnp.bfloat16),
                    pltpu.VMEM((steps * piece, wide), jnp.bfloat16),
                    pltpu.SemaphoreType.DMA((8,)),
                    pltpu.SemaphoreType.DMA((steps,)),
                ],
                compiler_params=FULL,
                cost_estimate=cost(flops, 1 << 20),
                name="project",
            )(after(place, *waits), *own, *peer, *blocks)
        else:
            *parts, later = begun
            parts = pl.pallas_call(
                late_kernel,
                out_shape=[pltpu.HBM(each.shape, each.dtype) for each in sums],
                grid=(1,),
                in_specs=[VMEM] * 6,
                out_specs=[pl.BlockSpec((2, count, middle), lambda i: (0, 0, 0))] * 4,
                compiler_params=PARAMS,
                cost_estimate=cost(flops // 4, 1 << 20),
                name="late",
            )(after(later, *waits), blocks[steps // 2], *parts)
        return parts

    def exchange(n, parts, waits):
        middle = chunks[n][1] * HD
        wide = 2 * middle
        kept_a, sent_a, kept_b, sent_b = parts
        near_a, near_b = to_chip(1, sent_a), to_chip(2, sent_b)
        near_a = after(near_a, *waits)
        second = pl.BlockSpec((1, count, middle), lambda i: (1, 0, 0))
        next_a, next_b = pl.pallas_call(
            fold_kernel,
            out_shape=[jax.ShapeDtypeStruct((count, middle), jnp.float32)] * 2,
            grid=(1,),
            in_specs=[second] * 4,
            out_specs=[all_of(count, middle)] * 2,
            compiler_params=PARAMS,
            cost_estimate=cost(2 * count * wide, 1 << 18),
            name="fold",
        )(kept_a, near_a, kept_b, near_b)
        return next_a, [kept_a, near_a, to_chip(2, next_a), kept_b, near_b, to_chip(1, next_b)]

    def rows_of(begin, shares, waits):
        wide = 2 * sum(share[2].shape[1] for share in shares)
        first_half = [
            pl.BlockSpec((1, count, share[2].shape[1]), lambda i: (0, 0, 0)) for share in shares
        ]
        specs = [
            [half, half, all_of(count, share[2].shape[1])] * 2
            for half, share in zip(first_half, shares)
        ]
        keyval, outgoing = pl.pallas_call(
            rows_kernel,
            out_shape=[
                pltpu.HBM((count, wide), jnp.bfloat16),
                pltpu.HBM((slots, wide), jnp.bfloat16),
            ],
            grid=(1,),
            in_specs=[all_of(1, wide), all_of(1, count)] + sum(specs, []),
            out_specs=[all_of(count, wide), all_of(slots, wide)],
            compiler_params=PARAMS,
            cost_estimate=cost(2 * slots * count * wide, 1 << 20),
            name="rows",
        )(after(kv_bias[None, begin : begin + wide], *waits), target[None, :], *sum(shares, []))
        return keyval, outgoing

    def send(begin, outgoing, stored):
        wide = outgoing.shape[1]
        received = lax.all_to_all(outgoing, ("fz", "fx"), split_axis=0, concat_axis=0, tiled=True)
        stored = pl.pallas_call(
            lambda *refs: refs[-1].__setitem__(Ellipsis, refs[0][...]),
            out_shape=jax.ShapeDtypeStruct((slots, columns), jnp.bfloat16),
            grid=(1,),
            in_specs=[all_of(slots, wide)] + [ANY] * len(stored),
            out_specs=pl.BlockSpec((slots, wide), lambda i: (0, begin // wide)),
            input_output_aliases={1: 0} if stored else {},
            compiler_params=PARAMS,
            cost_estimate=cost(1, 1 << 19),
            name="store",
        )(received, *stored)
        return stored

    def attend(begin, keyval, before):
        first, number = begin // (2 * HD), keyval.shape[1] // (2 * HD)
        return pl.pallas_call(
            functools.partial(attend_kernel, group=group),
            out_shape=jax.ShapeDtypeStruct(queries.shape, jnp.bfloat16),
            grid=(number,),
            in_specs=[
                pl.BlockSpec((count, group * HD), lambda i: (0, first + i)),
                pl.BlockSpec((count, 2 * HD), lambda i: (0, i)),
                all_of(count, HD),
                all_of(count, HD),
                all_of(count, 1),
            ]
            + [ANY] * len(before),
            out_specs=pl.BlockSpec((count, group * HD), lambda i: (0, first + i)),
            input_output_aliases={5: 0} if before else {},
            compiler_params=PARAMS,
            cost_estimate=cost(4 * number * group * count * count * HD, 1 << 20),
            name="attend",
        )(turned, keyval, cosine, sine, start[:, None], *before)

    parts_0 = add_up(0, None, (turned, target, start))
    gather(*chunks[1], relay=(parts_0[0],))
    gather(*chunks[2])
    begun = None
    if piece % HD == 0:
        wide = chunks[-1][1] * 2 * HD
        sums = [jax.ShapeDtypeStruct((2, count, wide // 2), jnp.float32)] * 4
        begun = begin_sums(gathered[-1], sums, wide)
    parts_1 = add_up(1, None, (parts_0[0],))
    _, share_0 = exchange(0, parts_0, (gathered[1][-1],))
    folded, share_1 = exchange(1, parts_1, (gathered[2][-1], *([] if begun is None else begun[:1])))
    split = chunks[1][0] * 2 * HD
    keyval, outgoing = rows_of(0, [share_0], (*([] if begun is None else begun[:1]),))
    attended = attend(0, keyval, [])
    parts_2 = add_up(2, begun, (keyval, folded))
    _, share_2 = exchange(2, parts_2, (attended,))
    stored = send(0, after(outgoing, parts_2[0]), [])
    keyval, outgoing = rows_of(split, [share_1, share_2], (attended,))
    stored = send(split, outgoing, [stored])
    return (attend(split, keyval, [attended]), stored)


def solution(mesh):
    groups, ranks, cores = (mesh.shape[name] for name in ("groups", "fsdp", "tp"))
    devices = mesh.devices.reshape(groups, ranks // 2, 2, cores)
    paired = jax.sharding.Mesh(devices, ("groups", "fz", "fx", "tp"))
    rows = ("groups", "fz", "fx")
    placed = (
        P(rows, "tp"),
        P(rows, "tp"),
        P(rows, None),
        P(rows, None),
        P("tp"),
        P(("fz", "fx"), "tp"),
        P("tp"),
    )
    return jax.shard_map(
        shards,
        mesh=paired,
        in_specs=placed,
        out_specs=(P(rows, "tp"), P(rows, "tp")),
        check_vma=False,
    )
```
